128 devices in a mesh: grp: 4 (over y_hi, core), st: 32 (over z, y_lo, x).
Axes of the slice: x: 4, y: 4 (y_hi: 2, y_lo: 2; y = y_hi * 2 + y_lo), z: 4, core: 2. Of those that a mesh axis runs over, the one named last changes fastest.
Arguments:
- start_vectors: float32 [32, 131072], P(None, ('grp', 'st')), may hold values from -6 to 6
- stay: float32 [131072], P(('grp', 'st')), may hold values from 0.1 to 0.6
- band_blocks: bfloat16 [131072, 8192], P(('grp', 'st')), may hold values from 0.0009994507 to 1
- band_start: int32 [512], P(('grp', 'st')), may hold values from -4096 to 126976, as said below
- band_width: int32 [512], P(('grp', 'st')), may hold values from 4096 to 8192, as said below
Outputs:
- vectors: float32 [32, 131072], P(None, ('grp', 'st'))
- ritz: float32 [32, 32], replicated
The draws below stay inside these ranges and needn't reach their ends.
Inputs may be any that keep to these rules, and one draw needn't show every extreme that they name: For band block b, band_start[b] - (b * 256 // 1024 - 4) * 1024 is a multiple of 128 from 0 to 1024; both ends occur in every draw. `band_width`: A multiple of 128; both ends occur in every draw.
All inputs are finite; a program needn't handle non-finite values.
Results may differ from the reference program's by a relative error of at most 0.0011.
Values may be sent and summed in bfloat16 or wider, within the bound.
A program may use at most 64 MiB of HBM per device.

```python
import math
import jax
import jax.numpy as jnp
from jax import lax

K = 32
CD = 1024
NEAR = 4
RB = 256
STEP = 128
ITERS = 12
BW = 8192
STATES = 131072
BLOCKS = 512


def draw_band_start(key, part):
    key = jax.random.fold_in(key, 11)
    block_index = jnp.arange(BLOCKS, dtype=jnp.int32)
    device_index = block_index * RB // CD
    offsets = jax.random.randint(key, (BLOCKS,), 0, CD // STEP + 1, dtype=jnp.int32)
    offsets = offsets.at[0].set(0)
    offsets = offsets.at[1].set(CD // STEP)
    offsets = offsets.at[BLOCKS - 1].set(CD // STEP)
    return ((device_index - NEAR) * CD + STEP * offsets).astype(jnp.int32)


def draw_band_width(key, part):
    key = jax.random.fold_in(key, 23)
    counts = jax.random.randint(key, (BLOCKS,), BW // (2 * STEP), BW // STEP + 1, dtype=jnp.int32)
    counts = counts.at[0].set(BW // STEP)
    counts = counts.at[1].set(BW // (2 * STEP))
    return (counts * STEP).astype(jnp.int32)


def block_levels(stream_key, shape, shards, low, largest):
    def one(axis_at, parts):
        steps = jax.random.uniform(jax.random.fold_in(jax.random.fold_in(stream_key, 6), axis_at), (parts,), jnp.float32, low / len(shards), largest / len(shards))
        return jnp.repeat(jnp.exp(steps), shape[axis_at] // parts).reshape((-1,) + (1,) * (len(shape) - axis_at - 1))

    gain = one(*shards[0])
    for cut in shards[1:]:
        gain = gain * one(*cut)
    return gain


def centred(stream_key, extent, width, bound, split=(), kind=jnp.bfloat16):
    entries = width * jax.random.normal(stream_key, extent, jnp.float32)
    if split:
        entries = entries * block_levels(stream_key, extent, split, -0.22, 0.18)
    return jnp.clip(entries, -bound, bound).astype(kind)


def setup_inputs(seed: int = 0) -> dict:
    keys = jax.random.split(jax.random.key(seed), 6)
    return {
        "start_vectors": centred(keys[0], (K, STATES), 1.0, 6.0, ((1, 128),), jnp.float32),
        "stay": jnp.clip(jnp.exp(math.log(0.6) - 1.7917595 * jax.random.uniform(keys[1], (STATES,), jnp.float32) ** block_levels(keys[1], (STATES,), ((0, 128),), -0.2, 0.2)), 0.1, 0.6),
        "band_blocks": jnp.clip(jnp.exp(math.log(1.0) - 6.9083047 * jax.random.uniform(keys[2], (STATES, BW), jnp.float32) ** block_levels(keys[2], (STATES, BW), ((0, 128),), -0.2, 0.2)), 0.0009994507, 1.0).astype(jnp.bfloat16),
        "band_start": draw_band_start(jax.random.fold_in(keys[5], 71), 0),
        "band_width": draw_band_width(jax.random.fold_in(keys[5], 71), 0),
    }


def band_device(padded, shaped, starts, widths):
    band_span = shaped.shape[2]

    def take_window(offset):
        return lax.dynamic_slice_in_dim(padded, offset + band_span, band_span, 1)
    windows = jax.vmap(take_window)(starts)
    columns = lax.broadcasted_iota(jnp.int32, (1, 1, band_span), 2)
    windows = jnp.where(columns < widths[:, None, None], windows, jnp.zeros((), jnp.bfloat16))
    terms = jnp.einsum('nkw,nrw->nkr', windows.astype(jnp.float32), shaped.astype(jnp.float32))
    return jnp.transpose(terms, (1, 0, 2)).reshape(terms.shape[1], -1)

def reference(start_vectors, stay, band_blocks, band_start, band_width):
    vector_count, state_count = start_vectors.shape
    band_span = band_blocks.shape[1]
    device_count = state_count // CD
    per_device = CD // RB
    shaped = band_blocks.reshape(device_count, per_device, RB, band_span)
    starts = band_start.reshape(device_count, per_device)
    widths = band_width.reshape(device_count, per_device)
    columns = lax.broadcasted_iota(jnp.int32, (1, 1, band_span), 2)

    def row_sums(pieces):
        block_rows, block_widths = pieces
        kept = jnp.where(columns < block_widths[:, None, None], block_rows.astype(jnp.float32), jnp.float32(0.0))
        return jnp.sum(kept, axis=2).reshape(-1)
    rowsum = lax.map(row_sums, (shaped, widths)).reshape(state_count)
    leave_scale = (1.0 - stay) / rowsum
    current = start_vectors
    ritz_matrix = jnp.zeros((vector_count, vector_count), jnp.float32)
    for step_index in range(ITERS):
        rounded = current.astype(jnp.bfloat16)
        padded = jnp.pad(rounded, ((0, 0), (band_span, band_span)))

        def per_dev(pieces):
            return band_device(padded, pieces[0], pieces[1], pieces[2])
        band_part = lax.map(per_dev, (shaped, starts, widths))
        band_part = jnp.transpose(band_part, (1, 0, 2)).reshape(vector_count, state_count)
        image = stay * current + leave_scale * band_part
        gram_matrix = jnp.dot(image, image.T, precision=lax.Precision.HIGHEST) / state_count
        ritz_matrix = jnp.dot(current, image.T, precision=lax.Precision.HIGHEST) / state_count
        lower_factor = jnp.linalg.cholesky(gram_matrix)
        current = lax.linalg.triangular_solve(lower_factor, image, left_side=True, lower=True)
    return (current, ritz_matrix)
```

```python
import functools

import jax
import jax.numpy as jnp
from jax import lax
from jax.experimental import pallas as pl
from jax.experimental.pallas import tpu as pltpu
from jax.sharding import PartitionSpec as P

ITERS = 12
MESH = pl.DeviceIdType.MESH
F32 = jnp.float32
BF16 = jnp.bfloat16
LANE = 128
SIZES = {"yh": 2, "core": 2, "z": 4, "yl": 2, "x": 4}
PHASES = (("yh", "yl", "x"), ("core", "z"))


def split3(value):
    high = value.astype(BF16)
    rest = value - high.astype(F32)
    mid = rest.astype(BF16)
    low = (rest - mid.astype(F32)).astype(BF16)
    return high, mid, low


def coordinates():
    grp, st = lax.axis_index("grp"), lax.axis_index("st")
    return {"yh": grp // 2, "core": grp % 2, "z": st // 8, "yl": (st // 4) % 2, "x": st % 4}


def device_of(at):
    return (at["yh"] * 2 + at["core"], at["z"] * 8 + at["yl"] * 4 + at["x"])


def group(at, names):
    place = 0
    for name in names:
        place = place * SIZES[name] + at[name]
    count = 1
    for name in names:
        count *= SIZES[name]
    others = []
    for code in range(1, count):
        peer, rest = dict(at), code
        for name in reversed(names):
            step = rest % SIZES[name]
            rest //= SIZES[name]
            if step:
                peer[name] = (at[name] + step) % SIZES[name]
        others.append(device_of(peer))
    return place, count, others


def tree_sum(items):
    items = list(items)
    while len(items) > 1:
        items = [a + b for a, b in zip(items[::2], items[1::2])] + ([items[-1]] if len(items) % 2 else [])
    return items[0]


def inverse_factor(gram_rows):
    shape = (8, LANE)
    row8 = lax.broadcasted_iota(jnp.int32, shape, 0)
    lane = lax.broadcasted_iota(jnp.int32, shape, 1)
    g = list(gram_rows)
    inv = [jnp.where(lane % 32 == row8 + 8 * q, F32(1), F32(0)) for q in range(4)]
    out = []
    for p in range(4):
        cols = [[jnp.broadcast_to(g[q][:, 8 * p + k : 8 * p + k + 1], shape) for q in range(p, 4)] for k in range(8)]
        diag = jnp.ones(shape, F32)
        for j in range(8):
            pivot = jnp.broadcast_to(cols[j][0][j : j + 1, :], shape)
            diag = jnp.where(row8 == j, pivot, diag)
            scale = 1.0 / pivot
            factors = [col * scale for col in cols[j]]
            factors[0] = jnp.where(row8 > j, factors[0], F32(0))
            for k in range(j + 1, 8):
                head = jnp.broadcast_to(cols[k][0][j : j + 1, :], shape)
                cols[k] = [col - factor * head for col, factor in zip(cols[k], factors)]
            row_g = jnp.broadcast_to(g[p][j : j + 1, :], shape)
            row_i = jnp.broadcast_to(inv[p][j : j + 1, :], shape)
            for q in range(p, 4):
                if q == p and j == 7:
                    continue
                if q > p or p < 3:
                    g[q] = g[q] - factors[q - p] * row_g
                inv[q] = inv[q] - factors[q - p] * row_i
        out.append(inv[p] * (1.0 / jnp.sqrt(diag)))
    return jnp.concatenate(out, axis=0)


def align(first_ref, width_ref, band_ref, weights, raw, sem):
    blocks, block_rows = raw.shape[0], raw.shape[1]
    window = weights.shape[0]
    loads = []
    for b in range(blocks):
        load = pltpu.make_async_copy(band_ref.at[pl.ds(b * block_rows, block_rows), :], raw.at[b], sem.at[b])
        load.start()
        loads.append(load)
    for b in range(blocks):
        here = slice(b * block_rows, (b + 1) * block_rows)
        loads[b].wait()
        first = first_ref[b] // LANE
        used = width_ref[b] // LANE

        def clear(e, carry, here=here):
            weights[pl.ds(pl.multiple_of(e * LANE, LANE), LANE), here] = jnp.zeros((LANE, block_rows), BF16)
            return carry

        def turn(e, carry, b=b, here=here, first=first):
            piece = raw[b, :, pl.ds(pl.multiple_of(e * LANE, LANE), LANE)]
            weights[pl.ds(pl.multiple_of((first + e) * LANE, LANE), LANE), here] = jnp.transpose(piece)
            return carry

        lax.fori_loop(0, first, clear, 0)
        lax.fori_loop(first + used, window // LANE, clear, 0)
        lax.fori_loop(0, used, turn, 0)


def kernel(
    start_ref, stay_ref, weights,
    out_ref, ritz_ref,
    xbuf, current, image, scale, acc,
    gram1, gram2, cross1, cross2,
    halo_send, halo_recv, send1, recv1, send2, recv2, csend, crecv,
):
    count, rows = start_ref.shape
    reach = (xbuf.shape[0] - 1) // 2
    devices = lax.axis_size("grp") * lax.axis_size("st")
    members = lax.axis_size("st")
    chain = lax.axis_index("grp") * members + lax.axis_index("st")
    at = coordinates()
    place1, count1, others1 = group(at, PHASES[0])
    place2, count2, others2 = group(at, PHASES[1])

    x = at["x"]

    def chained(by):
        there = lax.rem(chain + by + devices, devices)
        return (there // members, there % members)

    right = device_of({**at, "x": (x + 1) % 4})
    left = device_of({**at, "x": (x + 3) % 4})
    following, preceding = chained(4), chained(-4)
    neighbours = (right, left, following, preceding)

    barrier = pltpu.get_barrier_semaphore()
    for device in neighbours:
        pl.semaphore_signal(barrier, inc=1, device_id=device, device_id_type=MESH)
    for device in others1 + others2:
        pl.semaphore_signal(barrier, inc=1, device_id=device, device_id_type=MESH)

    current[...] = start_ref[...]
    xbuf[reach] = start_ref[...].astype(BF16)

    def pick(condition, first, second):
        return jnp.where(condition, reach + first, reach + second)

    def sending(which, arriving, src, dst, device):
        return pltpu.make_async_remote_copy(
            src_ref=src,
            dst_ref=dst,
            send_sem=halo_send.at[which],
            recv_sem=halo_recv.at[arriving],
            device_id=device,
            device_id_type=MESH,
        )

    def block_to(which, arriving, src, dst, device):
        return sending(which, arriving, xbuf.at[src], xbuf.at[dst], device)

    from_left, from_right = pick(x == 0, 3, -1), pick(x < 3, 1, -3)
    across = pick(x < 2, 2, -2)
    row_left, row_right = pick(x == 0, -1, 3), pick(x == 3, 1, -3)
    row_across = pick(x < 2, -2, 2)
    middle = jnp.logical_and(x >= 1, x <= 2)
    own = [
        block_to(2, 2, reach, reach - 4, following),
        block_to(3, 3, reach, reach + 4, preceding),
        block_to(0, 0, reach, pick(x == 3, 3, -1), right),
        block_to(1, 1, reach, pick(x >= 1, 1, -3), left),
    ]
    half = count // 2
    halves = []
    for which, src, first, dst, device in (
        (4, from_left, 0, pick(jnp.logical_or(x == 3, x == 0), 2, -2), right),
        (5, from_right, half, pick(middle, 2, -2), left),
    ):
        rows_of = pl.ds(first, half)
        halves.append(sending(which, which, xbuf.at[src, rows_of], xbuf.at[dst, rows_of], device))
    along = [
        block_to(6, 6, pick(x == 3, -4, 4), pick(x == 3, -1, 3), right),
        block_to(7, 7, pick(x >= 1, -4, 4), pick(x >= 1, -3, 1), left),
    ]
    onward = [
        block_to(8, 8, reach + 3, reach + 2, right),
        block_to(9, 8, reach - 3, reach - 2, left),
    ]

    def arrived(which, slot, rows_of=None):
        part = xbuf.at[slot] if rows_of is None else xbuf.at[slot, rows_of]
        pltpu.make_async_copy(part, part, halo_recv.at[which]).wait()

    pl.semaphore_wait(barrier, len(neighbours) + len(others1) + len(others2))
    for copy in own:
        copy.start()

    def stored(slot):
        return weights[pl.ds(pl.multiple_of(slot * rows, rows), rows), :]

    def product(slot):
        there = chain + (slot - reach)
        valid = jnp.where(jnp.logical_and(there >= 0, there < devices), F32(1), F32(0)).astype(BF16)
        return jnp.dot(xbuf[slot] * valid, stored(slot), preferred_element_type=F32)

    ones = jnp.ones((16, rows), BF16)
    sums = lax.fori_loop(
        0,
        2 * reach + 1,
        lambda slot, total: total + jnp.dot(ones, stored(slot), preferred_element_type=F32)[0:8],
        jnp.zeros((8, rows), F32),
    )
    scale[...] = (1.0 - stay_ref[...]) / sums[0:1]

    lane8 = lax.broadcasted_iota(jnp.int32, (8, LANE), 1) // 32
    lane32 = lax.broadcasted_iota(jnp.int32, (count, LANE), 1) // 32

    def packed_product(left3, right3):
        left = jnp.concatenate(left3, axis=0)
        right = jnp.concatenate([piece for piece in right3 for _ in range(4)], axis=0)
        terms = lax.dot_general(left, right, (((1,), (1,)), ((), ())), preferred_element_type=F32)
        full = tree_sum(terms[32 * a : 32 * a + 32, LANE * b : LANE * b + LANE] for a in (2, 1, 0) for b in (2, 1, 0))
        tile = full[0:8]
        for q in range(1, 4):
            tile = jnp.where(lane8 == q, full[8 * q : 8 * q + 8], tile)
        return tile * (1.0 / (rows * devices))

    def unpacked(tile):
        return [tile] + [pltpu.roll(tile, LANE - 32 * q, 1) for q in range(1, 4)]

    def send_all(buffer, place, others, send_sem, recv_sem):
        for device in others:
            pltpu.make_async_remote_copy(
                src_ref=buffer.at[place],
                dst_ref=buffer.at[place],
                send_sem=send_sem,
                recv_sem=recv_sem,
                device_id=device,
                device_id_type=MESH,
            ).start()

    def wait_all(buffer, others, sem):
        part = buffer.at[pl.ds(0, len(others))]
        pltpu.make_async_copy(part, part, sem).wait()

    def summed(buffer, n):
        return tree_sum(buffer[i] for i in range(n))

    def one_step(t, carry):
        parity = t % 2
        final = t == ITERS - 1
        acc[...] = product(reach)
        arrived(0, from_left)
        halves[0].start()
        arrived(1, from_right)
        halves[1].start()
        acc[...] += product(from_left) + product(from_right)
        arrived(2, reach - 4)
        arrived(3, reach + 4)
        for copy in along:
            copy.start()
        acc[...] += product(reach - 4) + product(reach + 4)
        arrived(4, across, pl.ds(0, half))
        arrived(5, across, pl.ds(half, half))
        acc[...] += product(across)
        arrived(6, row_left)
        arrived(7, row_right)

        @pl.when(middle)
        def _():
            for copy in onward:
                copy.start()

        acc[...] += product(row_left) + product(row_right)
        arrived(8, row_across)
        acc[...] += product(row_across)
        for copy in halves + along:
            copy.wait_send()

        @pl.when(middle)
        def _():
            for copy in onward:
                copy.wait_send()

        image[...] = stay_ref[...] * current[...] + scale[...] * acc[...]
        pieces = split3(image[...])
        buf1, buf2 = gram1.at[parity], gram2.at[parity]
        buf1[place1] = packed_product(pieces, pieces)
        send_all(buf1, place1, others1, send1, recv1.at[parity])

        @pl.when(final)
        def _():
            cross1[place1] = packed_product(split3(current[...]), pieces)
            send_all(cross1, place1, others1, csend.at[0], crecv.at[0])

        wait_all(buf1, others1, recv1.at[parity])
        buf2[place2] = summed(buf1, count1)
        send_all(buf2, place2, others2, send2, recv2.at[parity])

        @pl.when(final)
        def _():
            wait_all(cross1, others1, crecv.at[0])
            cross2[place2] = summed(cross1, count1)
            send_all(cross2, place2, others2, csend.at[1], crecv.at[1])

        wait_all(buf2, others2, recv2.at[parity])
        gram = unpacked(summed(buf2, count2))
        wait_all(buf1, others1, send1)
        wait_all(buf2, others2, send2)

        inverse = inverse_factor(gram)
        high, mid, low = (piece.astype(F32) for piece in split3(inverse))
        left_a = jnp.where(lane32 < 2, high, mid)
        left_b = jnp.where(lane32 == 0, high, jnp.where(lane32 == 2, mid, low))
        left = jnp.concatenate([left_a, left_b], axis=1).astype(BF16)
        ih, im, il = pieces
        right = jnp.concatenate([ih, im, ih, im, il, ih, il, im], axis=0)
        updated = jnp.dot(left, right, preferred_element_type=F32)
        current[...] = updated
        for copy in own:
            copy.wait_send()
        xbuf[reach] = updated.astype(BF16)

        @pl.when(jnp.logical_not(final))
        def _():
            for copy in own:
                copy.start()

        return carry

    lax.fori_loop(0, ITERS, one_step, 0)

    out_ref[...] = current[...]
    wait_all(cross2, others2, crecv.at[1])
    ritz = unpacked(summed(cross2, count2))
    for q in range(4):
        ritz_ref[8 * q : 8 * q + 8, :] = ritz[q][:, 0:32]
    wait_all(cross1, others1, csend.at[0])
    wait_all(cross2, others2, csend.at[1])


def shards(start_vectors, stay, band_blocks, band_start, band_width):
    count, rows = start_vectors.shape
    span = band_blocks.shape[1]
    blocks = band_start.shape[0]
    reach = span // (2 * rows)
    window = 2 * reach + 1
    vmem = pl.BlockSpec(memory_space=pltpu.VMEM)
    smem = pl.BlockSpec(memory_space=pltpu.SMEM)
    members1 = members2 = 1
    for name in PHASES[0]:
        members1 *= SIZES[name]
    for name in PHASES[1]:
        members2 *= SIZES[name]
    stay = stay.reshape(1, rows)
    chain = lax.axis_index("grp") * lax.axis_size("st") + lax.axis_index("st")
    first = band_start - (chain - reach) * rows
    weights = pl.pallas_call(
        align,
        out_shape=pltpu.VMEM((window * rows, rows), BF16),
        in_specs=[smem, smem, pl.BlockSpec(memory_space=pl.ANY)],
        out_specs=vmem,
        scratch_shapes=[pltpu.VMEM((blocks, rows // blocks, span), BF16), pltpu.SemaphoreType.DMA((blocks,))],
        compiler_params=pltpu.CompilerParams(vmem_limit_bytes=24 * 1024 * 1024),
        name="align",
    )(first, band_width, pltpu.with_memory_space_constraint(band_blocks, pltpu.HBM))
    weights = pltpu.with_memory_space_constraint(weights, pltpu.VMEM)
    return pl.pallas_call(
        kernel,
        out_shape=(jax.ShapeDtypeStruct((count, rows), F32), jax.ShapeDtypeStruct((count, count), F32)),
        in_specs=[vmem, vmem, vmem],
        out_specs=(vmem, vmem),
        scratch_shapes=[
            pltpu.VMEM((window, count, rows), BF16),
            pltpu.VMEM((count, rows), F32),
            pltpu.VMEM((count, rows), F32),
            pltpu.VMEM((1, rows), F32),
            pltpu.VMEM((count, rows), F32),
            pltpu.VMEM((2, members1, 8, LANE), F32),
            pltpu.VMEM((2, members2, 8, LANE), F32),
            pltpu.VMEM((members1, 8, LANE), F32),
            pltpu.VMEM((members2, 8, LANE), F32),
            pltpu.SemaphoreType.DMA((10,)),
            pltpu.SemaphoreType.DMA((9,)),
            pltpu.SemaphoreType.DMA,
            pltpu.SemaphoreType.DMA((2,)),
            pltpu.SemaphoreType.DMA,
            pltpu.SemaphoreType.DMA((2,)),
            pltpu.SemaphoreType.DMA((2,)),
            pltpu.SemaphoreType.DMA((2,)),
        ],
        compiler_params=pltpu.CompilerParams(
            collective_id=0, has_side_effects=True, vmem_limit_bytes=12 * 1024 * 1024
        ),
        name="subspace",
    )(start_vectors, stay, weights)


def solution(mesh):
    placed = (
        P(None, ("grp", "st")),
        P(("grp", "st")),
        P(("grp", "st"), None),
        P(("grp", "st")),
        P(("grp", "st")),
    )
    return jax.shard_map(
        shards, mesh=mesh, in_specs=placed, out_specs=(P(None, ("grp", "st")), P()), check_vma=False
    )
```

```python
import math

import jax
import jax.numpy as jnp
from jax import lax
from jax.experimental import pallas as pl
from jax.experimental.pallas import tpu as pltpu
from jax.sharding import PartitionSpec as P

ITERS = 12
MESH = pl.DeviceIdType.MESH
F32 = jnp.float32
BF16 = jnp.bfloat16
LANE = 128
SIZES = {"yh": 2, "core": 2, "z": 4, "yl": 2, "x": 4}
PHASES = (("yh", "yl", "x"), ("core", "z"))


def split3(value):
    high = value.astype(BF16)
    rest = value - high.astype(F32)
    mid = rest.astype(BF16)
    low = (rest - mid.astype(F32)).astype(BF16)
    return high, mid, low


def coordinates():
    grp, st = lax.axis_index("grp"), lax.axis_index("st")
    return {"yh": grp // 2, "core": grp % 2, "z": st // 8, "yl": (st // 4) % 2, "x": st % 4}


def device_of(at):
    return (at["yh"] * 2 + at["core"], at["z"] * 8 + at["yl"] * 4 + at["x"])


def group(at, names):
    place = 0
    for name in names:
        place = place * SIZES[name] + at[name]
    count = 1
    for name in names:
        count *= SIZES[name]
    others = []
    for code in range(1, count):
        peer, rest = dict(at), code
        for name in reversed(names):
            step = rest % SIZES[name]
            rest //= SIZES[name]
            if step:
                peer[name] = (at[name] + step) % SIZES[name]
        others.append(device_of(peer))
    return place, count, others


def tree_sum(items):
    items = list(items)
    while len(items) > 1:
        items = [a + b for a, b in zip(items[::2], items[1::2])] + ([items[-1]] if len(items) % 2 else [])
    return items[0]


def inverse_factor(gram_rows):
    shape = (8, LANE)
    row8 = lax.broadcasted_iota(jnp.int32, shape, 0)
    lane = lax.broadcasted_iota(jnp.int32, shape, 1)
    g = list(gram_rows)
    inv = [jnp.where(lane % 32 == row8 + 8 * q, F32(1), F32(0)) for q in range(4)]
    out = []
    for p in range(4):
        cols = [[jnp.broadcast_to(g[q][:, 8 * p + k : 8 * p + k + 1], shape) for q in range(p, 4)] for k in range(8)]
        diag = jnp.ones(shape, F32)
        for j in range(8):
            pivot = jnp.broadcast_to(cols[j][0][j : j + 1, :], shape)
            diag = jnp.where(row8 == j, pivot, diag)
            scale = 1.0 / pivot
            factors = [col * scale for col in cols[j]]
            factors[0] = jnp.where(row8 > j, factors[0], F32(0))
            for k in range(j + 1, 8):
                head = jnp.broadcast_to(cols[k][0][j : j + 1, :], shape)
                cols[k] = [col - factor * head for col, factor in zip(cols[k], factors)]
            row_g = jnp.broadcast_to(g[p][j : j + 1, :], shape)
            row_i = jnp.broadcast_to(inv[p][j : j + 1, :], shape)
            for q in range(p, 4):
                if q == p and j == 7:
                    continue
                if q > p or p < 3:
                    g[q] = g[q] - factors[q - p] * row_g
                inv[q] = inv[q] - factors[q - p] * row_i
        out.append(inv[p] * (1.0 / jnp.sqrt(diag)))
    return jnp.concatenate(out, axis=0)


def align(first_ref, width_ref, band_ref, weights, raw, sem):
    blocks, block_rows = raw.shape[0], raw.shape[1]
    window = weights.shape[0]
    loads = []
    for b in range(blocks):
        load = pltpu.make_async_copy(band_ref.at[pl.ds(b * block_rows, block_rows), :], raw.at[b], sem.at[b])
        load.start()
        loads.append(load)
    for b in range(blocks):
        here = slice(b * block_rows, (b + 1) * block_rows)
        loads[b].wait()
        first = first_ref[b] // LANE
        used = width_ref[b] // LANE

        def clear(e, carry, here=here):
            weights[pl.ds(pl.multiple_of(e * LANE, LANE), LANE), here] = jnp.zeros((LANE, block_rows), BF16)
            return carry

        def turn(e, carry, b=b, here=here, first=first):
            piece = raw[b, :, pl.ds(pl.multiple_of(e * LANE, LANE), LANE)]
            weights[pl.ds(pl.multiple_of((first + e) * LANE, LANE), LANE), here] = jnp.transpose(piece)
            return carry

        lax.fori_loop(0, raw.shape[2] // LANE, turn, 0, unroll=8)
        lax.fori_loop(0, first, clear, 0)
        lax.fori_loop(first + used, window // LANE, clear, 0)


def row_scale(stay_ref, weights, scale_ref):
    rows = stay_ref.shape[1]
    ones = jnp.ones((16, rows), BF16)
    total = jnp.zeros((8, rows), F32)
    for d in range(weights.shape[0] // rows):
        total += jnp.dot(ones, weights[d * rows : (d + 1) * rows, :], preferred_element_type=F32)[0:8]
    scale_ref[...] = (1.0 - stay_ref[...]) / total[0:1]


def kernel(
    start_ref, stay_ref, scale_ref, weights,
    out_ref, ritz_ref,
    images, xbuf, left_ref, current, acc,
    sums,
    bulk_send, bulk_recv, row_send, row_recv, sum_send, sum_recv,
):
    count, rows = start_ref.shape
    reach = weights.shape[0] // (2 * rows)
    devices = lax.axis_size("grp") * lax.axis_size("st")
    members = lax.axis_size("st")
    chain = lax.axis_index("grp") * members + lax.axis_index("st")
    at = coordinates()
    groups = [group(at, names) for names in PHASES]

    x = at["x"]

    def chained(by):
        there = lax.rem(chain + by + devices, devices)
        return (there // members, there % members)

    right = device_of({**at, "x": (x + 1) % 4})
    left = device_of({**at, "x": (x + 3) % 4})
    following, preceding = chained(4), chained(-4)
    across = device_of({**at, "x": (x + 2) % 4})
    neighbours = (right, left, across, following, preceding)

    barrier = pltpu.get_barrier_semaphore()
    for device in neighbours:
        pl.semaphore_signal(barrier, inc=1, device_id=device, device_id_type=MESH)
    for device in [device for _, _, others in groups for device in others]:
        pl.semaphore_signal(barrier, inc=1, device_id=device, device_id_type=MESH)

    def pick(condition, first, second):
        return jnp.where(condition, reach + first, reach + second)

    slots = (
        reach,
        pick(x == 0, 3, -1),
        pick(x < 3, 1, -3),
        pick(x < 2, 2, -2),
        reach - 4,
        reach + 4,
        pick(x == 0, -1, 3),
        pick(x == 3, 1, -3),
        pick(x < 2, -2, 2),
    )
    half = count // 2

    def remote(src, dst, send_sem, recv_sem, device):
        return pltpu.make_async_remote_copy(
            src_ref=src, dst_ref=dst, send_sem=send_sem, recv_sem=recv_sem, device_id=device, device_id_type=MESH
        )

    def spread(parity):
        return [
            remote(images.at[parity, 0], images.at[parity, to], bulk_send.at[k], bulk_recv.at[parity, k], device)
            for k, to, device in ((0, 4, following), (1, 5, preceding), (2, 1, right), (3, 2, left))
        ]

    def onward(parity):
        return [
            remote(
                images.at[parity, src, pl.ds(first, half)],
                images.at[parity, 3, pl.ds(first, half)],
                bulk_send.at[k],
                bulk_recv.at[parity, k],
                device,
            )
            for k, src, first, device in ((4, 1, 0, right), (5, 2, half, left))
        ]

    def arrived(parity, k, block, part=None):
        ref = images.at[parity, block] if part is None else images.at[parity, block, part]
        pltpu.make_async_copy(ref, ref, bulk_recv.at[parity, k]).wait()

    before, after = 4, 5
    along = [
        remote(xbuf.at[jnp.where(x >= 2, before, after)], xbuf.at[8], row_send.at[2], row_recv.at[2], across),
        remote(xbuf.at[jnp.where(x == 3, before, after)], xbuf.at[6], row_send.at[0], row_recv.at[0], right),
        remote(xbuf.at[jnp.where(x >= 1, before, after)], xbuf.at[7], row_send.at[1], row_recv.at[1], left),
    ]

    images[0, 0] = start_ref[...]
    row8 = lax.broadcasted_iota(jnp.int32, (count, 8 * count), 0)
    lane8 = lax.broadcasted_iota(jnp.int32, (count, 8 * count), 1)
    kept = jnp.logical_or(lane8 // 32 < 2, lane8 // 32 == 4)
    left_ref[...] = jnp.where(jnp.logical_and(kept, lane8 % 32 == row8), F32(1), F32(0)).astype(BF16)
    pl.semaphore_wait(barrier, len(neighbours) + sum(len(others) for _, _, others in groups))
    for copy in spread(0):
        copy.start()
    arrived(0, 2, 1)
    arrived(0, 3, 2)
    for copy in onward(0):
        copy.start()

    def stored(slot):
        return weights[pl.ds(pl.multiple_of(slot * rows, rows), rows), :]

    def product(block):
        there = chain + (slots[block] - reach)
        valid = jnp.where(jnp.logical_and(there >= 0, there < devices), F32(1), F32(0)).astype(BF16)
        return jnp.dot(xbuf[block] * valid, stored(slots[block]), preferred_element_type=F32)

    def orthonormal(image):
        ih, im, il = split3(image)
        right = jnp.concatenate([ih, im, ih, im, il, ih, il, im], axis=0)
        return jnp.dot(left_ref[...], right, preferred_element_type=F32)

    lane8 = lax.broadcasted_iota(jnp.int32, (8, LANE), 1) // 32
    lane32 = lax.broadcasted_iota(jnp.int32, (count, LANE), 1) // 32

    def packed_product(left3, right3):
        left = jnp.concatenate(left3, axis=0)
        right = jnp.concatenate([piece for piece in right3 for _ in range(4)], axis=0)
        terms = lax.dot_general(left, right, (((1,), (1,)), ((), ())), preferred_element_type=F32)
        full = tree_sum(terms[32 * a : 32 * a + 32, LANE * b : LANE * b + LANE] for a in (2, 1, 0) for b in (2, 1, 0))
        tile = full[0:8]
        for q in range(1, 4):
            tile = jnp.where(lane8 == q, full[8 * q : 8 * q + 8], tile)
        return tile * (1.0 / (rows * devices))

    def unpacked(tile):
        return [tile] + [pltpu.roll(tile, LANE - 32 * q, 1) for q in range(1, 4)]

    stages = len(groups)
    cross = 2 * stages

    def send_all(stage, base, tile):
        place, _, others = groups[stage]
        own_slot = sums.at[base + stage, place]
        own_slot[...] = tile
        for device in others:
            pltpu.make_async_remote_copy(
                src_ref=own_slot,
                dst_ref=own_slot,
                send_sem=sum_send.at[base + stage],
                recv_sem=sum_recv.at[base + stage],
                device_id=device,
                device_id_type=MESH,
            ).start()

    def wait_all(stage, base, sem):
        part = sums.at[base + stage, pl.ds(0, len(groups[stage][2]))]
        pltpu.make_async_copy(part, part, sem.at[base + stage]).wait()

    def received(stage, base):
        wait_all(stage, base, sum_recv)
        return tree_sum(sums[base + stage, i] for i in range(groups[stage][1]))

    def one_step(t, carry):
        parity = t % 2
        final = t == ITERS - 1
        arrived(parity, 0, 4)
        xbuf[4] = orthonormal(images[parity, 4]).astype(BF16)
        arrived(parity, 1, 5)
        xbuf[5] = orthonormal(images[parity, 5]).astype(BF16)
        for copy in along:
            copy.start()
        updated = orthonormal(images[parity, 0])
        current[...] = updated
        xbuf[0] = updated.astype(BF16)
        acc[...] = product(0) + product(4) + product(5)
        xbuf[1] = orthonormal(images[parity, 1]).astype(BF16)
        xbuf[2] = orthonormal(images[parity, 2]).astype(BF16)
        acc[...] += product(1) + product(2)
        arrived(parity, 4, 3, pl.ds(0, half))
        arrived(parity, 5, 3, pl.ds(half, half))
        xbuf[3] = orthonormal(images[parity, 3]).astype(BF16)
        acc[...] += product(3)
        for k, block in ((0, 6), (1, 7), (2, 8)):
            pltpu.make_async_copy(xbuf.at[block], xbuf.at[block], row_recv.at[k]).wait()
        acc[...] += product(6) + product(7) + product(8)
        for copy in spread(parity) + onward(parity) + along:
            copy.wait_send()

        image = stay_ref[...] * current[...] + scale_ref[...] * acc[...]
        images[1 - parity, 0] = image
        pieces = split3(image)
        base = parity * stages
        send_all(0, base, packed_product(pieces, pieces))

        @pl.when(jnp.logical_not(final))
        def _():
            for copy in spread(1 - parity):
                copy.start()

        @pl.when(final)
        def _():
            send_all(0, cross, packed_product(split3(current[...]), pieces))

        for stage in range(1, stages):
            send_all(stage, base, received(stage - 1, base))

            @pl.when(final)
            def _(stage=stage):
                send_all(stage, cross, received(stage - 1, cross))

        gram = unpacked(received(stages - 1, base))

        @pl.when(jnp.logical_not(final))
        def _():
            arrived(1 - parity, 2, 1)
            arrived(1 - parity, 3, 2)
            for copy in onward(1 - parity):
                copy.start()

        for stage in range(stages):
            wait_all(stage, base, sum_send)

        high, mid, low = (piece.astype(F32) for piece in split3(inverse_factor(gram)))
        left_a = jnp.where(lane32 < 2, high, mid)
        left_b = jnp.where(lane32 == 0, high, jnp.where(lane32 == 2, mid, low))
        left_ref[...] = jnp.concatenate([left_a, left_b], axis=1).astype(BF16)
        return carry

    lax.fori_loop(0, ITERS, one_step, 0)

    out_ref[...] = orthonormal(images[ITERS % 2, 0])
    ritz = unpacked(received(stages - 1, cross))
    for q in range(4):
        ritz_ref[8 * q : 8 * q + 8, :] = ritz[q][:, 0:32]
    for stage in range(stages):
        wait_all(stage, cross, sum_send)


def shards(start_vectors, stay, band_blocks, band_start, band_width):
    count, rows = start_vectors.shape
    span = band_blocks.shape[1]
    blocks = band_start.shape[0]
    reach = span // (2 * rows)
    window = 2 * reach + 1
    vmem = pl.BlockSpec(memory_space=pltpu.VMEM)
    smem = pl.BlockSpec(memory_space=pltpu.SMEM)
    most = max(math.prod(SIZES[name] for name in names) for names in PHASES)
    stay = stay.reshape(1, rows)
    chain = lax.axis_index("grp") * lax.axis_size("st") + lax.axis_index("st")
    first = band_start - (chain - reach) * rows
    weights = pl.pallas_call(
        align,
        out_shape=pltpu.VMEM((window * rows, rows), BF16),
        in_specs=[smem, smem, pl.BlockSpec(memory_space=pl.ANY)],
        out_specs=vmem,
        scratch_shapes=[pltpu.VMEM((blocks, rows // blocks, span), BF16), pltpu.SemaphoreType.DMA((blocks,))],
        compiler_params=pltpu.CompilerParams(vmem_limit_bytes=24 * 1024 * 1024),
        name="align",
    )(first, band_width, pltpu.with_memory_space_constraint(band_blocks, pltpu.HBM))
    weights = pltpu.with_memory_space_constraint(weights, pltpu.VMEM)
    scale = pl.pallas_call(
        row_scale,
        out_shape=jax.ShapeDtypeStruct((1, rows), F32),
        in_specs=[vmem, vmem],
        out_specs=vmem,
        compiler_params=pltpu.CompilerParams(vmem_limit_bytes=8 * 1024 * 1024),
        name="row_scale",
    )(stay, weights)
    return pl.pallas_call(
        kernel,
        out_shape=(jax.ShapeDtypeStruct((count, rows), F32), jax.ShapeDtypeStruct((count, count), F32)),
        in_specs=[vmem, vmem, vmem, vmem],
        out_specs=(vmem, vmem),
        scratch_shapes=[
            pltpu.VMEM((2, 6, count, rows), F32),
            pltpu.VMEM((window, count, rows), BF16),
            pltpu.VMEM((count, 8 * count), BF16),
            pltpu.VMEM((count, rows), F32),
            pltpu.VMEM((count, rows), F32),
            pltpu.VMEM((3 * len(PHASES), most, 8, LANE), F32),
            pltpu.SemaphoreType.DMA((6,)),
            pltpu.SemaphoreType.DMA((2, 6)),
            pltpu.SemaphoreType.DMA((3,)),
            pltpu.SemaphoreType.DMA((3,)),
            pltpu.SemaphoreType.DMA((3 * len(PHASES),)),
            pltpu.SemaphoreType.DMA((3 * len(PHASES),)),
        ],
        compiler_params=pltpu.CompilerParams(
            collective_id=0, has_side_effects=True, vmem_limit_bytes=12 * 1024 * 1024
        ),
        name="subspace",
    )(start_vectors, stay, scale, weights)


def solution(mesh):
    placed = (
        P(None, ("grp", "st")),
        P(("grp", "st")),
        P(("grp", "st"), None),
        P(("grp", "st")),
        P(("grp", "st")),
    )
    return jax.shard_map(
        shards, mesh=mesh, in_specs=placed, out_specs=(P(None, ("grp", "st")), P()), check_vma=False
    )
```

```python
import math

import jax
import jax.numpy as jnp
from jax import lax
from jax.experimental import pallas as pl
from jax.experimental.pallas import tpu as pltpu
from jax.sharding import PartitionSpec as P

ITERS = 12
MESH = pl.DeviceIdType.MESH
F32 = jnp.float32
BF16 = jnp.bfloat16
LANE = 128
SIZES = {"yh": 2, "core": 2, "z": 4, "yl": 2, "x": 4}
PHASES = (("yh", "yl", "x"), ("core", "z"))


def split3(value):
    high = value.astype(BF16)
    rest = value - high.astype(F32)
    mid = rest.astype(BF16)
    low = (rest - mid.astype(F32)).astype(BF16)
    return high, mid, low


def coordinates():
    grp, st = lax.axis_index("grp"), lax.axis_index("st")
    return {"yh": grp // 2, "core": grp % 2, "z": st // 8, "yl": (st // 4) % 2, "x": st % 4}


def device_of(at):
    return (at["yh"] * 2 + at["core"], at["z"] * 8 + at["yl"] * 4 + at["x"])


def group(at, names):
    place = 0
    for name in names:
        place = place * SIZES[name] + at[name]
    count = 1
    for name in names:
        count *= SIZES[name]
    others = []
    for code in range(1, count):
        peer, rest = dict(at), code
        for name in reversed(names):
            step = rest % SIZES[name]
            rest //= SIZES[name]
            if step:
                peer[name] = (at[name] + step) % SIZES[name]
        others.append(device_of(peer))
    return place, count, others


def tree_sum(items):
    items = list(items)
    while len(items) > 1:
        items = [a + b for a, b in zip(items[::2], items[1::2])] + ([items[-1]] if len(items) % 2 else [])
    return items[0]


def inverse_factor(gram_rows):
    shape = (8, LANE)
    row8 = lax.broadcasted_iota(jnp.int32, shape, 0)
    lane = lax.broadcasted_iota(jnp.int32, shape, 1)
    g = list(gram_rows)
    inv = [jnp.where(lane % 32 == row8 + 8 * q, F32(1), F32(0)) for q in range(4)]
    out = []
    for p in range(4):
        cols = [[jnp.broadcast_to(g[q][:, 8 * p + k : 8 * p + k + 1], shape) for q in range(p, 4)] for k in range(8)]
        diag = jnp.ones(shape, F32)
        for j in range(8):
            pivot = jnp.broadcast_to(cols[j][0][j : j + 1, :], shape)
            diag = jnp.where(row8 == j, pivot, diag)
            scale = 1.0 / pivot
            factors = [col * scale for col in cols[j]]
            factors[0] = jnp.where(row8 > j, factors[0], F32(0))
            for k in range(j + 1, 8):
                head = jnp.broadcast_to(cols[k][0][j : j + 1, :], shape)
                cols[k] = [col - factor * head for col, factor in zip(cols[k], factors)]
            row_g = jnp.broadcast_to(g[p][j : j + 1, :], shape)
            row_i = jnp.broadcast_to(inv[p][j : j + 1, :], shape)
            for q in range(p, 4):
                if q == p and j == 7:
                    continue
                if q > p or p < 3:
                    g[q] = g[q] - factors[q - p] * row_g
                inv[q] = inv[q] - factors[q - p] * row_i
        out.append(inv[p] * (1.0 / jnp.sqrt(diag)))
    return jnp.concatenate(out, axis=0)


def align(stay_ref, first_ref, width_ref, band_ref, weights, scale_ref, raw, sem):
    chunks, chunk_rows = raw.shape[0], raw.shape[1]
    window = weights.shape[0]
    ahead = 3
    loads = [
        pltpu.make_async_copy(band_ref.at[pl.ds(c * chunk_rows, chunk_rows), :], raw.at[c], sem.at[c])
        for c in range(chunks)
    ]
    for c in range(ahead):
        loads[c].start()
    for c in range(chunks):
        here = slice(c * chunk_rows, (c + 1) * chunk_rows)
        loads[c].wait()
        if c + ahead < chunks:
            loads[c + ahead].start()
        block = c * first_ref.shape[0] // chunks
        first = first_ref[block] // LANE
        used = width_ref[block] // LANE

        def clear(e, carry, here=here):
            weights[pl.ds(pl.multiple_of(e * LANE, LANE), LANE), here] = jnp.zeros((LANE, chunk_rows), BF16)
            return carry

        def turn(e, total, c=c, here=here, first=first, used=used):
            piece = jnp.transpose(raw[c, :, pl.ds(pl.multiple_of(e * LANE, LANE), LANE)])
            weights[pl.ds(pl.multiple_of((first + e) * LANE, LANE), LANE), here] = piece
            part = tree_sum(piece[r : r + 16].astype(F32) for r in range(0, LANE, 16))
            return total + jnp.where(e < used, part, F32(0))

        total = lax.fori_loop(0, raw.shape[2] // LANE, turn, jnp.zeros((16, chunk_rows), F32), unroll=8)
        lax.fori_loop(0, first, clear, 0)
        lax.fori_loop(first + used, window // LANE, clear, 0)
        scale_ref[:, here] = (1.0 - stay_ref[:, here]) / jnp.sum(total, axis=0, keepdims=True)


def kernel(
    start_ref, stay_ref, scale_ref, weights,
    out_ref, ritz_ref,
    images, xbuf, left_ref, current, acc,
    sums,
    bulk_send, bulk_recv, row_send, row_recv, sum_send, sum_recv,
):
    count, rows = start_ref.shape
    reach = weights.shape[0] // (2 * rows)
    devices = lax.axis_size("grp") * lax.axis_size("st")
    members = lax.axis_size("st")
    chain = lax.axis_index("grp") * members + lax.axis_index("st")
    at = coordinates()
    groups = [group(at, names) for names in PHASES]

    x = at["x"]

    def chained(by):
        there = lax.rem(chain + by + devices, devices)
        return (there // members, there % members)

    right = device_of({**at, "x": (x + 1) % 4})
    left = device_of({**at, "x": (x + 3) % 4})
    following, preceding = chained(4), chained(-4)
    neighbours = (right, left, following, preceding)

    barrier = pltpu.get_barrier_semaphore()
    for device in neighbours:
        pl.semaphore_signal(barrier, inc=1, device_id=device, device_id_type=MESH)
    for device in [device for _, _, others in groups for device in others]:
        pl.semaphore_signal(barrier, inc=1, device_id=device, device_id_type=MESH)

    def pick(condition, first, second):
        return jnp.where(condition, reach + first, reach + second)

    slots = (
        reach,
        pick(x == 0, 3, -1),
        pick(x < 3, 1, -3),
        pick(x < 2, 2, -2),
        reach - 4,
        reach + 4,
        pick(x == 0, -1, 3),
        pick(x == 3, 1, -3),
        pick(x < 2, -2, 2),
    )
    half = count // 2

    def remote(src, dst, send_sem, recv_sem, device):
        return pltpu.make_async_remote_copy(
            src_ref=src, dst_ref=dst, send_sem=send_sem, recv_sem=recv_sem, device_id=device, device_id_type=MESH
        )

    def spread(parity):
        return [
            remote(images.at[parity, 0], images.at[parity, to], bulk_send.at[k], bulk_recv.at[parity, k], device)
            for k, to, device in ((2, 1, right), (3, 2, left), (0, 4, following), (1, 5, preceding))
        ]

    def onward(parity):
        return [
            remote(
                images.at[parity, src, pl.ds(first, half)],
                images.at[parity, 3, pl.ds(first, half)],
                bulk_send.at[k],
                bulk_recv.at[parity, k],
                device,
            )
            for k, src, first, device in ((4, 1, 0, right), (5, 2, half, left))
        ]

    def arrived(parity, k, block, part=None):
        ref = images.at[parity, block] if part is None else images.at[parity, block, part]
        pltpu.make_async_copy(ref, ref, bulk_recv.at[parity, k]).wait()

    before, after = 4, 5
    along = [
        remote(xbuf.at[jnp.where(x == 3, before, after)], xbuf.at[6], row_send.at[0], row_recv.at[0], right),
        remote(xbuf.at[jnp.where(x >= 1, before, after)], xbuf.at[7], row_send.at[1], row_recv.at[1], left),
    ]
    same_x = tuple(jnp.where(x < 2, a, b) for a, b in zip(following, preceding))
    over = remote(xbuf.at[3], xbuf.at[8], row_send.at[2], row_recv.at[2], same_x)

    images[0, 0] = start_ref[...]
    row8 = lax.broadcasted_iota(jnp.int32, (count, 8 * count), 0)
    lane8 = lax.broadcasted_iota(jnp.int32, (count, 8 * count), 1)
    kept = jnp.logical_or(lane8 // 32 < 2, lane8 // 32 == 4)
    left_ref[...] = jnp.where(jnp.logical_and(kept, lane8 % 32 == row8), F32(1), F32(0)).astype(BF16)
    pl.semaphore_wait(barrier, len(neighbours) + sum(len(others) for _, _, others in groups))
    for copy in spread(0):
        copy.start()
    arrived(0, 2, 1)
    arrived(0, 3, 2)
    for copy in onward(0):
        copy.start()

    def stored(slot):
        return weights[pl.ds(pl.multiple_of(slot * rows, rows), rows), :]

    def product(block):
        there = chain + (slots[block] - reach)
        valid = jnp.where(jnp.logical_and(there >= 0, there < devices), F32(1), F32(0)).astype(BF16)
        return jnp.dot(xbuf[block] * valid, stored(slots[block]), preferred_element_type=F32)

    def orthonormal(image):
        ih, im, il = split3(image)
        right = jnp.concatenate([ih, im, ih, im, il, ih, il, im], axis=0)
        return jnp.dot(left_ref[...], right, preferred_element_type=F32)

    lane8 = lax.broadcasted_iota(jnp.int32, (8, LANE), 1) // 32
    lane32 = lax.broadcasted_iota(jnp.int32, (count, LANE), 1) // 32

    def packed_product(left3, right3):
        left = jnp.concatenate(left3, axis=0)
        right = jnp.concatenate([piece for piece in right3 for _ in range(4)], axis=0)
        terms = lax.dot_general(left, right, (((1,), (1,)), ((), ())), preferred_element_type=F32)
        full = tree_sum(terms[32 * a : 32 * a + 32, LANE * b : LANE * b + LANE] for a in (2, 1, 0) for b in (2, 1, 0))
        tile = full[0:8]
        for q in range(1, 4):
            tile = jnp.where(lane8 == q, full[8 * q : 8 * q + 8], tile)
        return tile * (1.0 / (rows * devices))

    def unpacked(tile):
        return [tile] + [pltpu.roll(tile, LANE - 32 * q, 1) for q in range(1, 4)]

    stages = len(groups)
    cross = 2 * stages

    def send_all(stage, base, tile):
        place, _, others = groups[stage]
        own_slot = sums.at[base + stage, place]
        own_slot[...] = tile
        for device in others:
            pltpu.make_async_remote_copy(
                src_ref=own_slot,
                dst_ref=own_slot,
                send_sem=sum_send.at[base + stage],
                recv_sem=sum_recv.at[base + stage],
                device_id=device,
                device_id_type=MESH,
            ).start()

    def wait_all(stage, base, sem):
        part = sums.at[base + stage, pl.ds(0, len(groups[stage][2]))]
        pltpu.make_async_copy(part, part, sem.at[base + stage]).wait()

    def received(stage, base):
        wait_all(stage, base, sum_recv)
        return tree_sum(sums[base + stage, i] for i in range(groups[stage][1]))

    def one_step(t, carry):
        parity = t % 2
        final = t == ITERS - 1
        arrived(parity, 0, 4)
        arrived(parity, 1, 5)
        xbuf[4] = orthonormal(images[parity, 4]).astype(BF16)
        xbuf[5] = orthonormal(images[parity, 5]).astype(BF16)
        for copy in along:
            copy.start()
        updated = orthonormal(images[parity, 0])
        current[...] = updated
        xbuf[0] = updated.astype(BF16)
        arrived(parity, 4, 3, pl.ds(0, half))
        arrived(parity, 5, 3, pl.ds(half, half))
        xbuf[3] = orthonormal(images[parity, 3]).astype(BF16)
        over.start()
        xbuf[1] = orthonormal(images[parity, 1]).astype(BF16)
        xbuf[2] = orthonormal(images[parity, 2]).astype(BF16)
        acc[...] = tree_sum(product(block) for block in range(6))
        for k, block in ((0, 6), (1, 7)):
            pltpu.make_async_copy(xbuf.at[block], xbuf.at[block], row_recv.at[k]).wait()
        acc[...] += product(6) + product(7)
        pltpu.make_async_copy(xbuf.at[8], xbuf.at[8], row_recv.at[2]).wait()
        acc[...] += product(8)
        for copy in spread(parity) + onward(parity) + along + [over]:
            copy.wait_send()

        image = stay_ref[...] * current[...] + scale_ref[...] * acc[...]
        images[1 - parity, 0] = image
        pieces = split3(image)
        base = parity * stages
        send_all(0, base, packed_product(pieces, pieces))

        @pl.when(jnp.logical_not(final))
        def _():
            for copy in spread(1 - parity):
                copy.start()

        @pl.when(final)
        def _():
            send_all(0, cross, packed_product(split3(current[...]), pieces))

        for stage in range(1, stages):
            send_all(stage, base, received(stage - 1, base))

            @pl.when(final)
            def _(stage=stage):
                send_all(stage, cross, received(stage - 1, cross))

        gram = unpacked(received(stages - 1, base))

        @pl.when(jnp.logical_not(final))
        def _():
            arrived(1 - parity, 2, 1)
            arrived(1 - parity, 3, 2)
            for copy in onward(1 - parity):
                copy.start()

        for stage in range(stages):
            wait_all(stage, base, sum_send)

        high, mid, low = (piece.astype(F32) for piece in split3(inverse_factor(gram)))
        left_a = jnp.where(lane32 < 2, high, mid)
        left_b = jnp.where(lane32 == 0, high, jnp.where(lane32 == 2, mid, low))
        left_ref[...] = jnp.concatenate([left_a, left_b], axis=1).astype(BF16)
        return carry

    lax.fori_loop(0, ITERS, one_step, 0)

    out_ref[...] = orthonormal(images[ITERS % 2, 0])
    ritz = unpacked(received(stages - 1, cross))
    for q in range(4):
        ritz_ref[8 * q : 8 * q + 8, :] = ritz[q][:, 0:32]
    for stage in range(stages):
        wait_all(stage, cross, sum_send)


def shards(start_vectors, stay, band_blocks, band_start, band_width):
    count, rows = start_vectors.shape
    span = band_blocks.shape[1]
    blocks = band_start.shape[0]
    reach = span // (2 * rows)
    window = 2 * reach + 1
    vmem = pl.BlockSpec(memory_space=pltpu.VMEM)
    smem = pl.BlockSpec(memory_space=pltpu.SMEM)
    most = max(math.prod(SIZES[name] for name in names) for names in PHASES)
    stay = stay.reshape(1, rows)
    chain = lax.axis_index("grp") * lax.axis_size("st") + lax.axis_index("st")
    first = band_start - (chain - reach) * rows
    weights, scale = pl.pallas_call(
        align,
        out_shape=(pltpu.VMEM((window * rows, rows), BF16), jax.ShapeDtypeStruct((1, rows), F32)),
        in_specs=[vmem, smem, smem, pl.BlockSpec(memory_space=pl.ANY)],
        out_specs=(vmem, vmem),
        scratch_shapes=[pltpu.VMEM((8, rows // 8, span), BF16), pltpu.SemaphoreType.DMA((8,))],
        compiler_params=pltpu.CompilerParams(vmem_limit_bytes=24 * 1024 * 1024),
        name="align",
    )(stay, first, band_width, pltpu.with_memory_space_constraint(band_blocks, pltpu.HBM))
    weights = pltpu.with_memory_space_constraint(weights, pltpu.VMEM)
    return pl.pallas_call(
        kernel,
        out_shape=(jax.ShapeDtypeStruct((count, rows), F32), jax.ShapeDtypeStruct((count, count), F32)),
        in_specs=[vmem, vmem, vmem, vmem],
        out_specs=(vmem, vmem),
        scratch_shapes=[
            pltpu.VMEM((2, 6, count, rows), F32),
            pltpu.VMEM((window, count, rows), BF16),
            pltpu.VMEM((count, 8 * count), BF16),
            pltpu.VMEM((count, rows), F32),
            pltpu.VMEM((count, rows), F32),
            pltpu.VMEM((3 * len(PHASES), most, 8, LANE), F32),
            pltpu.SemaphoreType.DMA((6,)),
            pltpu.SemaphoreType.DMA((2, 6)),
            pltpu.SemaphoreType.DMA((3,)),
            pltpu.SemaphoreType.DMA((3,)),
            pltpu.SemaphoreType.DMA((3 * len(PHASES),)),
            pltpu.SemaphoreType.DMA((3 * len(PHASES),)),
        ],
        compiler_params=pltpu.CompilerParams(
            collective_id=0, has_side_effects=True, vmem_limit_bytes=12 * 1024 * 1024
        ),
        name="subspace",
    )(start_vectors, stay, scale, weights)


def solution(mesh):
    placed = (
        P(None, ("grp", "st")),
        P(("grp", "st")),
        P(("grp", "st"), None),
        P(("grp", "st")),
        P(("grp", "st")),
    )
    return jax.shard_map(
        shards, mesh=mesh, in_specs=placed, out_specs=(P(None, ("grp", "st")), P()), check_vma=False
    )
```

```python
import math

import jax
import jax.numpy as jnp
from jax import lax
from jax.experimental import pallas as pl
from jax.experimental.pallas import tpu as pltpu
from jax.sharding import PartitionSpec as P

ITERS = 12
MESH = pl.DeviceIdType.MESH
F32 = jnp.float32
BF16 = jnp.bfloat16
LANE = 128
SIZES = {"yh": 2, "core": 2, "z": 4, "yl": 2, "x": 4}
PHASES = (("yh", "yl", "x"), ("core", "z"))


def split3(value):
    high = value.astype(BF16)
    rest = value - high.astype(F32)
    mid = rest.astype(BF16)
    low = (rest - mid.astype(F32)).astype(BF16)
    return high, mid, low


def coordinates():
    grp, st = lax.axis_index("grp"), lax.axis_index("st")
    return {"yh": grp // 2, "core": grp % 2, "z": st // 8, "yl": (st // 4) % 2, "x": st % 4}


def device_of(at):
    return (at["yh"] * 2 + at["core"], at["z"] * 8 + at["yl"] * 4 + at["x"])


def group(at, names):
    place = 0
    for name in names:
        place = place * SIZES[name] + at[name]
    count = 1
    for name in names:
        count *= SIZES[name]
    others = []
    for code in range(1, count):
        peer, rest = dict(at), code
        for name in reversed(names):
            step = rest % SIZES[name]
            rest //= SIZES[name]
            if step:
                peer[name] = (at[name] + step) % SIZES[name]
        others.append(device_of(peer))
    return place, count, others


def tree_sum(items):
    items = list(items)
    while len(items) > 1:
        items = [a + b for a, b in zip(items[::2], items[1::2])] + ([items[-1]] if len(items) % 2 else [])
    return items[0]


def inverse_factor(gram_rows, midway):
    shape = (8, LANE)
    row8 = lax.broadcasted_iota(jnp.int32, shape, 0)
    lane = lax.broadcasted_iota(jnp.int32, shape, 1)
    g = list(gram_rows)
    inv = [jnp.where(lane % 32 == row8 + 8 * q, F32(1), F32(0)) for q in range(4)]
    out = []
    for p in range(4):
        if p == 2:
            midway()
        cols = [[jnp.broadcast_to(g[q][:, 8 * p + k : 8 * p + k + 1], shape) for q in range(p, 4)] for k in range(8)]
        diag = jnp.ones(shape, F32)
        for j in range(8):
            pivot = jnp.broadcast_to(cols[j][0][j : j + 1, :], shape)
            diag = jnp.where(row8 == j, pivot, diag)
            scale = 1.0 / pivot
            factors = [col * scale for col in cols[j]]
            factors[0] = jnp.where(row8 > j, factors[0], F32(0))
            for k in range(j + 1, 8):
                head = jnp.broadcast_to(cols[k][0][j : j + 1, :], shape)
                cols[k] = [col - factor * head for col, factor in zip(cols[k], factors)]
            row_g = jnp.broadcast_to(g[p][j : j + 1, :], shape)
            row_i = jnp.broadcast_to(inv[p][j : j + 1, :], shape)
            for q in range(p, 4):
                if q == p and j == 7:
                    continue
                if q > p or p < 3:
                    g[q] = g[q] - factors[q - p] * row_g
                inv[q] = inv[q] - factors[q - p] * row_i
        out.append(inv[p] * (1.0 / jnp.sqrt(diag)))
    return jnp.concatenate(out, axis=0)


def align(start_ref, width_ref, band_ref, weights, raw, starts, widths, sem, small_sem):
    blocks, block_rows = raw.shape[0], raw.shape[1]
    window, rows = weights.shape
    chain = lax.axis_index("grp") * lax.axis_size("st") + lax.axis_index("st")
    ahead, pieces = 2, 2
    part = block_rows // pieces
    loads = [
        pltpu.make_async_copy(
            band_ref.at[pl.ds(k * part, part), :], raw.at[k // pieces, pl.ds((k % pieces) * part, part)], sem.at[k]
        )
        for k in range(blocks * pieces)
    ]
    for load in loads[:ahead]:
        load.start()
    small = [
        pltpu.make_async_copy(start_ref, starts, small_sem.at[0]),
        pltpu.make_async_copy(width_ref, widths, small_sem.at[1]),
    ]
    for copy in small:
        copy.start()
    for copy in small:
        copy.wait()
    for b in range(blocks):
        here = slice(b * block_rows, (b + 1) * block_rows)
        for k in range(b * pieces, (b + 1) * pieces):
            loads[k].wait()
            if k + ahead < len(loads):
                loads[k + ahead].start()
        first = (starts[b] - chain * rows) // LANE + (window - rows) // (2 * LANE)
        used = widths[b] // LANE

        def clear(e, carry, here=here):
            weights[pl.ds(pl.multiple_of(e * LANE, LANE), LANE), here] = jnp.zeros((LANE, block_rows), BF16)
            return carry

        def turn(e, carry, b=b, here=here, first=first):
            piece = raw[b, :, pl.ds(pl.multiple_of(e * LANE, LANE), LANE)]
            weights[pl.ds(pl.multiple_of((first + e) * LANE, LANE), LANE), here] = jnp.transpose(piece)
            return carry

        lax.fori_loop(0, raw.shape[2] // LANE, turn, 0, unroll=8)
        lax.fori_loop(0, first, clear, 0)
        lax.fori_loop(first + used, window // LANE, clear, 0)


def row_sums(weights, sums_ref):
    rows = sums_ref.shape[1]
    ones = jnp.ones((16, rows), BF16)
    total = jnp.zeros((8, rows), F32)
    for d in range(weights.shape[0] // rows):
        total += jnp.dot(ones, weights[d * rows : (d + 1) * rows, :], preferred_element_type=F32)[0:8]
    sums_ref[...] = total[0:1]


def kernel(
    start_ref, stay_in, rowsum_ref, weights,
    out_ref, ritz_ref,
    stay_ref, scale_ref, images, xbuf, left_ref, current, acc,
    sums,
    bulk_send, bulk_recv, row_send, row_recv, sum_send, sum_recv, input_sem,
):
    count, rows = start_ref.shape
    reach = weights.shape[0] // (2 * rows)
    devices = lax.axis_size("grp") * lax.axis_size("st")
    members = lax.axis_size("st")
    chain = lax.axis_index("grp") * members + lax.axis_index("st")
    at = coordinates()
    groups = [group(at, names) for names in PHASES]

    inputs = [
        pltpu.make_async_copy(start_ref, images.at[0, 0], input_sem.at[0]),
        pltpu.make_async_copy(stay_in, stay_ref, input_sem.at[1]),
    ]
    for copy in inputs:
        copy.start()

    x = at["x"]

    def chained(by):
        there = lax.rem(chain + by + devices, devices)
        return (there // members, there % members)

    right = device_of({**at, "x": (x + 1) % 4})
    left = device_of({**at, "x": (x + 3) % 4})
    following, preceding = chained(4), chained(-4)
    across = device_of({**at, "x": (x + 2) % 4})
    neighbours = (right, left, across, following, preceding)

    barrier = pltpu.get_barrier_semaphore()
    for device in neighbours:
        pl.semaphore_signal(barrier, inc=1, device_id=device, device_id_type=MESH)
    for device in [device for _, _, others in groups for device in others]:
        pl.semaphore_signal(barrier, inc=1, device_id=device, device_id_type=MESH)

    def pick(condition, first, second):
        return jnp.where(condition, reach + first, reach + second)

    slots = (
        reach,
        pick(x == 0, 3, -1),
        pick(x < 3, 1, -3),
        pick(x < 2, 2, -2),
        reach - 4,
        reach + 4,
        pick(x == 0, -1, 3),
        pick(x == 3, 1, -3),
        pick(x < 2, -2, 2),
    )
    half = count // 2

    def remote(src, dst, send_sem, recv_sem, device):
        return pltpu.make_async_remote_copy(
            src_ref=src, dst_ref=dst, send_sem=send_sem, recv_sem=recv_sem, device_id=device, device_id_type=MESH
        )

    def spread(parity):
        return [
            remote(images.at[parity, 0], images.at[parity, to], bulk_send.at[k], bulk_recv.at[parity, k], device)
            for k, to, device in ((0, 4, following), (1, 5, preceding), (2, 1, right), (3, 2, left))
        ]

    def onward(parity):
        return [
            remote(
                images.at[parity, src, pl.ds(first, half)],
                images.at[parity, 3, pl.ds(first, half)],
                bulk_send.at[k],
                bulk_recv.at[parity, k],
                device,
            )
            for k, src, first, device in ((4, 1, 0, right), (5, 2, half, left))
        ]

    def arrived(parity, k, block, part=None):
        ref = images.at[parity, block] if part is None else images.at[parity, block, part]
        pltpu.make_async_copy(ref, ref, bulk_recv.at[parity, k]).wait()

    before, after = 4, 5
    along = [
        remote(xbuf.at[jnp.where(x >= 2, before, after)], xbuf.at[8], row_send.at[2], row_recv.at[2], across),
        remote(xbuf.at[jnp.where(x == 3, before, after)], xbuf.at[6], row_send.at[0], row_recv.at[0], right),
        remote(xbuf.at[jnp.where(x >= 1, before, after)], xbuf.at[7], row_send.at[1], row_recv.at[1], left),
    ]

    row8 = lax.broadcasted_iota(jnp.int32, (count, 8 * count), 0)
    lane8 = lax.broadcasted_iota(jnp.int32, (count, 8 * count), 1)
    kept = jnp.logical_or(lane8 // 32 < 2, lane8 // 32 == 4)
    left_ref[...] = jnp.where(jnp.logical_and(kept, lane8 % 32 == row8), F32(1), F32(0)).astype(BF16)
    pl.semaphore_wait(barrier, len(neighbours) + sum(len(others) for _, _, others in groups))
    for copy in inputs:
        copy.wait()
    for copy in spread(0):
        copy.start()
    scale_ref[...] = (1.0 - stay_ref[...]) / rowsum_ref[...]
    arrived(0, 2, 1)
    arrived(0, 3, 2)
    for copy in onward(0):
        copy.start()

    def stored(slot):
        return weights[pl.ds(pl.multiple_of(slot * rows, rows), rows), :]

    def product(block):
        there = chain + (slots[block] - reach)
        valid = jnp.where(jnp.logical_and(there >= 0, there < devices), F32(1), F32(0)).astype(BF16)
        return jnp.dot(xbuf[block] * valid, stored(slots[block]), preferred_element_type=F32)

    def orthonormal(image):
        ih, im, il = split3(image)
        right = jnp.concatenate([ih, im, ih, im, il, ih, il, im], axis=0)
        return jnp.dot(left_ref[...], right, preferred_element_type=F32)

    lane8 = lax.broadcasted_iota(jnp.int32, (8, LANE), 1) // 32
    lane32 = lax.broadcasted_iota(jnp.int32, (count, LANE), 1) // 32

    def packed_product(left3, right3):
        left = jnp.concatenate(left3, axis=0)
        right = jnp.concatenate([piece for piece in right3 for _ in range(4)], axis=0)
        terms = lax.dot_general(left, right, (((1,), (1,)), ((), ())), preferred_element_type=F32)
        full = tree_sum(terms[32 * a : 32 * a + 32, LANE * b : LANE * b + LANE] for a in (2, 1, 0) for b in (2, 1, 0))
        tile = full[0:8]
        for q in range(1, 4):
            tile = jnp.where(lane8 == q, full[8 * q : 8 * q + 8], tile)
        return tile * (1.0 / (rows * devices))

    def unpacked(tile):
        return [tile] + [pltpu.roll(tile, LANE - 32 * q, 1) for q in range(1, 4)]

    stages = len(groups)
    cross = 2 * stages

    def send_all(stage, base, tile):
        place, _, others = groups[stage]
        own_slot = sums.at[base + stage, place]
        own_slot[...] = tile
        for device in others:
            pltpu.make_async_remote_copy(
                src_ref=own_slot,
                dst_ref=own_slot,
                send_sem=sum_send.at[base + stage],
                recv_sem=sum_recv.at[base + stage],
                device_id=device,
                device_id_type=MESH,
            ).start()

    def wait_all(stage, base, sem):
        part = sums.at[base + stage, pl.ds(0, len(groups[stage][2]))]
        pltpu.make_async_copy(part, part, sem.at[base + stage]).wait()

    def received(stage, base):
        wait_all(stage, base, sum_recv)
        return tree_sum(sums[base + stage, i] for i in range(groups[stage][1]))

    def one_step(t, carry):
        parity = t % 2
        final = t == ITERS - 1
        arrived(parity, 0, 4)
        xbuf[4] = orthonormal(images[parity, 4]).astype(BF16)
        arrived(parity, 1, 5)
        xbuf[5] = orthonormal(images[parity, 5]).astype(BF16)
        for copy in along:
            copy.start()
        updated = orthonormal(images[parity, 0])
        current[...] = updated
        xbuf[0] = updated.astype(BF16)
        acc[...] = product(0) + product(4) + product(5)
        xbuf[1] = orthonormal(images[parity, 1]).astype(BF16)
        xbuf[2] = orthonormal(images[parity, 2]).astype(BF16)
        acc[...] += product(1) + product(2)
        arrived(parity, 4, 3, pl.ds(0, half))
        arrived(parity, 5, 3, pl.ds(half, half))
        xbuf[3] = orthonormal(images[parity, 3]).astype(BF16)
        acc[...] += product(3)
        for k, block in ((0, 6), (1, 7), (2, 8)):
            pltpu.make_async_copy(xbuf.at[block], xbuf.at[block], row_recv.at[k]).wait()
        acc[...] += product(6) + product(7) + product(8)
        for copy in spread(parity) + onward(parity) + along:
            copy.wait_send()

        image = stay_ref[...] * current[...] + scale_ref[...] * acc[...]
        images[1 - parity, 0] = image
        pieces = split3(image)
        base = parity * stages
        early = spread(1 - parity)

        @pl.when(jnp.logical_not(final))
        def _():
            for copy in early[:2]:
                copy.start()

        send_all(0, base, packed_product(pieces, pieces))

        @pl.when(jnp.logical_not(final))
        def _():
            for copy in early[2:]:
                copy.start()

        @pl.when(final)
        def _():
            send_all(0, cross, packed_product(split3(current[...]), pieces))

        for stage in range(1, stages):
            send_all(stage, base, received(stage - 1, base))

            @pl.when(final)
            def _(stage=stage):
                send_all(stage, cross, received(stage - 1, cross))

        gram = unpacked(received(stages - 1, base))

        def pass_on():
            @pl.when(jnp.logical_not(final))
            def _():
                arrived(1 - parity, 2, 1)
                arrived(1 - parity, 3, 2)
                for copy in onward(1 - parity):
                    copy.start()

        for stage in range(stages):
            wait_all(stage, base, sum_send)

        high, mid, low = (piece.astype(F32) for piece in split3(inverse_factor(gram, pass_on)))
        left_a = jnp.where(lane32 < 2, high, mid)
        left_b = jnp.where(lane32 == 0, high, jnp.where(lane32 == 2, mid, low))
        left_ref[...] = jnp.concatenate([left_a, left_b], axis=1).astype(BF16)
        return carry

    lax.fori_loop(0, ITERS, one_step, 0)

    out_ref[...] = orthonormal(images[ITERS % 2, 0])
    ritz = unpacked(received(stages - 1, cross))
    for q in range(4):
        ritz_ref[8 * q : 8 * q + 8, :] = ritz[q][:, 0:32]
    for stage in range(stages):
        wait_all(stage, cross, sum_send)


def shards(start_vectors, stay, band_blocks, band_start, band_width):
    count, rows = start_vectors.shape
    span = band_blocks.shape[1]
    blocks = band_start.shape[0]
    reach = span // (2 * rows)
    window = 2 * reach + 1
    vmem = pl.BlockSpec(memory_space=pltpu.VMEM)
    most = max(math.prod(SIZES[name] for name in names) for names in PHASES)
    stay = stay.reshape(1, rows)
    hbm = pl.BlockSpec(memory_space=pl.ANY)

    def held(array):
        return pltpu.with_memory_space_constraint(array, pltpu.HBM)

    weights = pl.pallas_call(
        align,
        out_shape=pltpu.VMEM((window * rows, rows), BF16),
        in_specs=[hbm, hbm, hbm],
        out_specs=vmem,
        scratch_shapes=[
            pltpu.VMEM((blocks, rows // blocks, span), BF16),
            pltpu.SMEM((blocks,), jnp.int32),
            pltpu.SMEM((blocks,), jnp.int32),
            pltpu.SemaphoreType.DMA((2 * blocks,)),
            pltpu.SemaphoreType.DMA((2,)),
        ],
        compiler_params=pltpu.CompilerParams(vmem_limit_bytes=24 * 1024 * 1024),
        name="align",
    )(held(band_start), held(band_width), held(band_blocks))
    weights = pltpu.with_memory_space_constraint(weights, pltpu.VMEM)
    rowsum = pl.pallas_call(
        row_sums,
        out_shape=jax.ShapeDtypeStruct((1, rows), F32),
        in_specs=[vmem],
        out_specs=vmem,
        compiler_params=pltpu.CompilerParams(vmem_limit_bytes=8 * 1024 * 1024),
        name="row_sums",
    )(weights)
    return pl.pallas_call(
        kernel,
        out_shape=(jax.ShapeDtypeStruct((count, rows), F32), jax.ShapeDtypeStruct((count, count), F32)),
        in_specs=[hbm, hbm, vmem, vmem],
        out_specs=(vmem, vmem),
        scratch_shapes=[
            pltpu.VMEM((1, rows), F32),
            pltpu.VMEM((1, rows), F32),
            pltpu.VMEM((2, 6, count, rows), F32),
            pltpu.VMEM((window, count, rows), BF16),
            pltpu.VMEM((count, 8 * count), BF16),
            pltpu.VMEM((count, rows), F32),
            pltpu.VMEM((count, rows), F32),
            pltpu.VMEM((3 * len(PHASES), most, 8, LANE), F32),
            pltpu.SemaphoreType.DMA((6,)),
            pltpu.SemaphoreType.DMA((2, 6)),
            pltpu.SemaphoreType.DMA((3,)),
            pltpu.SemaphoreType.DMA((3,)),
            pltpu.SemaphoreType.DMA((3 * len(PHASES),)),
            pltpu.SemaphoreType.DMA((3 * len(PHASES),)),
            pltpu.SemaphoreType.DMA((2,)),
        ],
        compiler_params=pltpu.CompilerParams(
            collective_id=0, has_side_effects=True, vmem_limit_bytes=12 * 1024 * 1024
        ),
        name="subspace",
    )(held(start_vectors), held(stay), rowsum, weights)


def solution(mesh):
    placed = (
        P(None, ("grp", "st")),
        P(("grp", "st")),
        P(("grp", "st"), None),
        P(("grp", "st")),
        P(("grp", "st")),
    )
    return jax.shard_map(
        shards, mesh=mesh, in_specs=placed, out_specs=(P(None, ("grp", "st")), P()), check_vma=False
    )
```

```python
import math

import jax
import jax.numpy as jnp
from jax import lax
from jax.experimental import pallas as pl
from jax.experimental.pallas import tpu as pltpu
from jax.sharding import PartitionSpec as P

ITERS = 12
MESH = pl.DeviceIdType.MESH
F32 = jnp.float32
BF16 = jnp.bfloat16
LANE = 128
SIZES = {"yh": 2, "core": 2, "z": 4, "yl": 2, "x": 4}
PHASES = (("yh", "yl", "x"), ("core", "z"))


def split3(value):
    high = value.astype(BF16)
    rest = value - high.astype(F32)
    mid = rest.astype(BF16)
    low = (rest - mid.astype(F32)).astype(BF16)
    return high, mid, low


def coordinates():
    grp, st = lax.axis_index("grp"), lax.axis_index("st")
    return {"yh": grp // 2, "core": grp % 2, "z": st // 8, "yl": (st // 4) % 2, "x": st % 4}


def device_of(at):
    return (at["yh"] * 2 + at["core"], at["z"] * 8 + at["yl"] * 4 + at["x"])


def group(at, names):
    place = 0
    for name in names:
        place = place * SIZES[name] + at[name]
    count = 1
    for name in names:
        count *= SIZES[name]
    others = []
    for code in range(1, count):
        peer, rest = dict(at), code
        for name in reversed(names):
            step = rest % SIZES[name]
            rest //= SIZES[name]
            if step:
                peer[name] = (at[name] + step) % SIZES[name]
        others.append(device_of(peer))
    return place, count, others


def tree_sum(items):
    items = list(items)
    while len(items) > 1:
        items = [a + b for a, b in zip(items[::2], items[1::2])] + ([items[-1]] if len(items) % 2 else [])
    return items[0]


def inverse_factor(gram_rows, midway):
    shape = (8, LANE)
    row8 = lax.broadcasted_iota(jnp.int32, shape, 0)
    lane = lax.broadcasted_iota(jnp.int32, shape, 1)
    g = list(gram_rows)
    inv = [jnp.where(lane % 32 == row8 + 8 * q, F32(1), F32(0)) for q in range(4)]

    def whole(tile, i):
        return jnp.broadcast_to(tile[i : i + 1, :], shape)

    out = []
    for p in range(4):
        if p == 2:
            midway()
        cols = [[jnp.broadcast_to(g[q][:, 8 * p + k : 8 * p + k + 1], shape) for q in range(p, 4)] for k in range(8)]
        e = {(i, k): whole(cols[k][0], i) for k in range(8) for i in range(k, 8)}
        rows_g = [whole(g[p], i) for i in range(8)] if p < 3 else []
        rows_i = [whole(inv[p], i) for i in range(8)]
        m, scale = {}, []
        for j in range(8):
            scale.append(1.0 / e[j, j])
            for i in range(j + 1, 8):
                m[i, j] = e[i, j] * scale[j]
            for k in range(j + 1, 8):
                for i in range(k, 8):
                    e[i, k] = e[i, k] - m[i, j] * e[k, j]
        n = {}
        for i in range(8):
            for j in range(i):
                total = m[i, j]
                for k in range(j + 1, i):
                    total = total + m[i, k] * n[k, j]
                n[i, j] = -total

        def finished(rows):
            done = []
            for i in range(8):
                total = rows[i]
                for j in range(i):
                    total = total + n[i, j] * rows[j]
                done.append(total)
            return done

        done_g, done_i = finished(rows_g) if p < 3 else [], finished(rows_i)
        for q in range(p + 1, 4):
            below = [cols[k][q - p] for k in range(8)]
            change_g, change_i = [], []
            for j in range(8):
                factor = below[j] * scale[j]
                for k in range(j + 1, 8):
                    below[k] = below[k] - factor * e[k, j]
                change_g.append(factor * done_g[j])
                change_i.append(factor * done_i[j])
            g[q] = g[q] - tree_sum(change_g)
            inv[q] = inv[q] - tree_sum(change_i)
        rows_done, diag = done_i[0], e[0, 0]
        for j in range(1, 8):
            rows_done = jnp.where(row8 == j, done_i[j], rows_done)
            diag = jnp.where(row8 == j, e[j, j], diag)
        out.append(rows_done * (1.0 / jnp.sqrt(diag)))
    return jnp.concatenate(out, axis=0)


def align(start_ref, width_ref, band_ref, weights, raw, starts, widths, sem, small_sem):
    blocks, block_rows = raw.shape[0], raw.shape[1]
    window, rows = weights.shape
    chain = lax.axis_index("grp") * lax.axis_size("st") + lax.axis_index("st")
    ahead, pieces = 2, 2
    part = block_rows // pieces
    loads = [
        pltpu.make_async_copy(
            band_ref.at[pl.ds(k * part, part), :], raw.at[k // pieces, pl.ds((k % pieces) * part, part)], sem.at[k]
        )
        for k in range(blocks * pieces)
    ]
    for load in loads[:ahead]:
        load.start()
    small = [
        pltpu.make_async_copy(start_ref, starts, small_sem.at[0]),
        pltpu.make_async_copy(width_ref, widths, small_sem.at[1]),
    ]
    for copy in small:
        copy.start()
    for copy in small:
        copy.wait()
    for b in range(blocks):
        here = slice(b * block_rows, (b + 1) * block_rows)
        for k in range(b * pieces, (b + 1) * pieces):
            loads[k].wait()
            if k + ahead < len(loads):
                loads[k + ahead].start()
        first = (starts[b] - chain * rows) // LANE + (window - rows) // (2 * LANE)
        used = widths[b] // LANE

        def clear(e, carry, here=here):
            weights[pl.ds(pl.multiple_of(e * LANE, LANE), LANE), here] = jnp.zeros((LANE, block_rows), BF16)
            return carry

        def turn(e, carry, b=b, here=here, first=first):
            piece = raw[b, :, pl.ds(pl.multiple_of(e * LANE, LANE), LANE)]
            weights[pl.ds(pl.multiple_of((first + e) * LANE, LANE), LANE), here] = jnp.transpose(piece)
            return carry

        lax.fori_loop(0, raw.shape[2] // LANE, turn, 0, unroll=8)
        lax.fori_loop(0, first, clear, 0)
        lax.fori_loop(first + used, window // LANE, clear, 0)


def row_sums(weights, sums_ref):
    rows = sums_ref.shape[1]
    ones = jnp.ones((16, rows), BF16)
    total = jnp.zeros((8, rows), F32)
    for d in range(weights.shape[0] // rows):
        total += jnp.dot(ones, weights[d * rows : (d + 1) * rows, :], preferred_element_type=F32)[0:8]
    sums_ref[...] = total[0:1]


def kernel(
    start_ref, stay_in, rowsum_ref, weights,
    out_ref, ritz_ref,
    stay_ref, scale_ref, images, xbuf, left_ref, current, acc,
    sums,
    bulk_send, bulk_recv, row_send, row_recv, sum_send, sum_recv, input_sem,
):
    count, rows = start_ref.shape
    reach = weights.shape[0] // (2 * rows)
    devices = lax.axis_size("grp") * lax.axis_size("st")
    members = lax.axis_size("st")
    chain = lax.axis_index("grp") * members + lax.axis_index("st")
    at = coordinates()
    groups = [group(at, names) for names in PHASES]

    inputs = [
        pltpu.make_async_copy(start_ref, images.at[0, 0], input_sem.at[0]),
        pltpu.make_async_copy(stay_in, stay_ref, input_sem.at[1]),
    ]
    for copy in inputs:
        copy.start()

    x = at["x"]

    def chained(by):
        there = lax.rem(chain + by + devices, devices)
        return (there // members, there % members)

    right = device_of({**at, "x": (x + 1) % 4})
    left = device_of({**at, "x": (x + 3) % 4})
    following, preceding = chained(4), chained(-4)
    across = device_of({**at, "x": (x + 2) % 4})
    neighbours = (right, left, across, following, preceding)

    barrier = pltpu.get_barrier_semaphore()
    for device in neighbours:
        pl.semaphore_signal(barrier, inc=1, device_id=device, device_id_type=MESH)
    for device in [device for _, _, others in groups for device in others]:
        pl.semaphore_signal(barrier, inc=1, device_id=device, device_id_type=MESH)

    def pick(condition, first, second):
        return jnp.where(condition, reach + first, reach + second)

    slots = (
        reach,
        pick(x == 0, 3, -1),
        pick(x < 3, 1, -3),
        pick(x < 2, 2, -2),
        reach - 4,
        reach + 4,
        pick(x == 0, -1, 3),
        pick(x == 3, 1, -3),
        pick(x < 2, -2, 2),
    )
    half = count // 2

    def remote(src, dst, send_sem, recv_sem, device):
        return pltpu.make_async_remote_copy(
            src_ref=src, dst_ref=dst, send_sem=send_sem, recv_sem=recv_sem, device_id=device, device_id_type=MESH
        )

    def spread(parity):
        return [
            remote(images.at[parity, 0], images.at[parity, to], bulk_send.at[k], bulk_recv.at[parity, k], device)
            for k, to, device in ((0, 4, following), (1, 5, preceding), (2, 1, right), (3, 2, left))
        ]

    def onward(parity):
        return [
            remote(
                images.at[parity, src, pl.ds(first, half)],
                images.at[parity, 3, pl.ds(first, half)],
                bulk_send.at[k],
                bulk_recv.at[parity, k],
                device,
            )
            for k, src, first, device in ((4, 1, 0, right), (5, 2, half, left))
        ]

    def arrived(parity, k, block, part=None):
        ref = images.at[parity, block] if part is None else images.at[parity, block, part]
        pltpu.make_async_copy(ref, ref, bulk_recv.at[parity, k]).wait()

    before, after = 4, 5
    along = [
        remote(xbuf.at[jnp.where(x >= 2, before, after)], xbuf.at[8], row_send.at[2], row_recv.at[2], across),
        remote(xbuf.at[jnp.where(x == 3, before, after)], xbuf.at[6], row_send.at[0], row_recv.at[0], right),
        remote(xbuf.at[jnp.where(x >= 1, before, after)], xbuf.at[7], row_send.at[1], row_recv.at[1], left),
    ]

    row8 = lax.broadcasted_iota(jnp.int32, (count, 8 * count), 0)
    lane8 = lax.broadcasted_iota(jnp.int32, (count, 8 * count), 1)
    kept = jnp.logical_or(lane8 // 32 < 2, lane8 // 32 == 4)
    left_ref[...] = jnp.where(jnp.logical_and(kept, lane8 % 32 == row8), F32(1), F32(0)).astype(BF16)
    pl.semaphore_wait(barrier, len(neighbours) + sum(len(others) for _, _, others in groups))
    for copy in inputs:
        copy.wait()
    for copy in spread(0):
        copy.start()
    scale_ref[...] = (1.0 - stay_ref[...]) / rowsum_ref[...]
    arrived(0, 2, 1)
    arrived(0, 3, 2)
    for copy in onward(0):
        copy.start()

    def stored(slot):
        return weights[pl.ds(pl.multiple_of(slot * rows, rows), rows), :]

    def product(block):
        there = chain + (slots[block] - reach)
        valid = jnp.where(jnp.logical_and(there >= 0, there < devices), F32(1), F32(0)).astype(BF16)
        return jnp.dot(xbuf[block] * valid, stored(slots[block]), preferred_element_type=F32)

    def orthonormal(image):
        ih, im, il = split3(image)
        right = jnp.concatenate([ih, im, ih, im, il, ih, il, im], axis=0)
        return jnp.dot(left_ref[...], right, preferred_element_type=F32)

    lane8 = lax.broadcasted_iota(jnp.int32, (8, LANE), 1) // 32
    lane32 = lax.broadcasted_iota(jnp.int32, (count, LANE), 1) // 32

    def packed_product(left3, right3):
        left = jnp.concatenate(left3, axis=0)
        right = jnp.concatenate([piece for piece in right3 for _ in range(4)], axis=0)
        terms = lax.dot_general(left, right, (((1,), (1,)), ((), ())), preferred_element_type=F32)
        full = tree_sum(terms[32 * a : 32 * a + 32, LANE * b : LANE * b + LANE] for a in (2, 1, 0) for b in (2, 1, 0))
        tile = full[0:8]
        for q in range(1, 4):
            tile = jnp.where(lane8 == q, full[8 * q : 8 * q + 8], tile)
        return tile * (1.0 / (rows * devices))

    def unpacked(tile):
        return [tile] + [pltpu.roll(tile, LANE - 32 * q, 1) for q in range(1, 4)]

    stages = len(groups)
    cross = 2 * stages

    def send_all(stage, base, tile):
        place, _, others = groups[stage]
        own_slot = sums.at[base + stage, place]
        own_slot[...] = tile
        for device in others:
            pltpu.make_async_remote_copy(
                src_ref=own_slot,
                dst_ref=own_slot,
                send_sem=sum_send.at[base + stage],
                recv_sem=sum_recv.at[base + stage],
                device_id=device,
                device_id_type=MESH,
            ).start()

    def wait_all(stage, base, sem):
        part = sums.at[base + stage, pl.ds(0, len(groups[stage][2]))]
        pltpu.make_async_copy(part, part, sem.at[base + stage]).wait()

    def received(stage, base):
        wait_all(stage, base, sum_recv)
        return tree_sum(sums[base + stage, i] for i in range(groups[stage][1]))

    def one_step(t, carry):
        parity = t % 2
        final = t == ITERS - 1
        arrived(parity, 0, 4)
        xbuf[4] = orthonormal(images[parity, 4]).astype(BF16)
        arrived(parity, 1, 5)
        xbuf[5] = orthonormal(images[parity, 5]).astype(BF16)
        for copy in along:
            copy.start()
        updated = orthonormal(images[parity, 0])
        current[...] = updated
        xbuf[0] = updated.astype(BF16)
        acc[...] = product(0) + product(4) + product(5)
        xbuf[1] = orthonormal(images[parity, 1]).astype(BF16)
        xbuf[2] = orthonormal(images[parity, 2]).astype(BF16)
        acc[...] += product(1) + product(2)
        arrived(parity, 4, 3, pl.ds(0, half))
        arrived(parity, 5, 3, pl.ds(half, half))
        xbuf[3] = orthonormal(images[parity, 3]).astype(BF16)
        acc[...] += product(3)
        for k, block in ((0, 6), (1, 7), (2, 8)):
            pltpu.make_async_copy(xbuf.at[block], xbuf.at[block], row_recv.at[k]).wait()
        acc[...] += product(6) + product(7) + product(8)
        for copy in spread(parity) + onward(parity) + along:
            copy.wait_send()

        image = stay_ref[...] * current[...] + scale_ref[...] * acc[...]
        images[1 - parity, 0] = image
        pieces = split3(image)
        base = parity * stages
        early = spread(1 - parity)

        send_all(0, base, packed_product(pieces, pieces))

        @pl.when(jnp.logical_not(final))
        def _():
            for copy in early:
                copy.start()

        @pl.when(final)
        def _():
            send_all(0, cross, packed_product(split3(current[...]), pieces))

        for stage in range(1, stages):
            send_all(stage, base, received(stage - 1, base))

            @pl.when(final)
            def _(stage=stage):
                send_all(stage, cross, received(stage - 1, cross))

        gram = unpacked(received(stages - 1, base))

        def pass_on():
            @pl.when(jnp.logical_not(final))
            def _():
                arrived(1 - parity, 2, 1)
                arrived(1 - parity, 3, 2)
                for copy in onward(1 - parity):
                    copy.start()

        for stage in range(stages):
            wait_all(stage, base, sum_send)

        high, mid, low = (piece.astype(F32) for piece in split3(inverse_factor(gram, pass_on)))
        left_a = jnp.where(lane32 < 2, high, mid)
        left_b = jnp.where(lane32 == 0, high, jnp.where(lane32 == 2, mid, low))
        left_ref[...] = jnp.concatenate([left_a, left_b], axis=1).astype(BF16)
        return carry

    lax.fori_loop(0, ITERS, one_step, 0)

    out_ref[...] = orthonormal(images[ITERS % 2, 0])
    ritz = unpacked(received(stages - 1, cross))
    for q in range(4):
        ritz_ref[8 * q : 8 * q + 8, :] = ritz[q][:, 0:32]
    for stage in range(stages):
        wait_all(stage, cross, sum_send)


def shards(start_vectors, stay, band_blocks, band_start, band_width):
    count, rows = start_vectors.shape
    span = band_blocks.shape[1]
    blocks = band_start.shape[0]
    reach = span // (2 * rows)
    window = 2 * reach + 1
    vmem = pl.BlockSpec(memory_space=pltpu.VMEM)
    most = max(math.prod(SIZES[name] for name in names) for names in PHASES)
    stay = stay.reshape(1, rows)
    hbm = pl.BlockSpec(memory_space=pl.ANY)

    def held(array):
        return pltpu.with_memory_space_constraint(array, pltpu.HBM)

    weights = pl.pallas_call(
        align,
        out_shape=pltpu.VMEM((window * rows, rows), BF16),
        in_specs=[hbm, hbm, hbm],
        out_specs=vmem,
        scratch_shapes=[
            pltpu.VMEM((blocks, rows // blocks, span), BF16),
            pltpu.SMEM((blocks,), jnp.int32),
            pltpu.SMEM((blocks,), jnp.int32),
            pltpu.SemaphoreType.DMA((2 * blocks,)),
            pltpu.SemaphoreType.DMA((2,)),
        ],
        compiler_params=pltpu.CompilerParams(vmem_limit_bytes=24 * 1024 * 1024),
        name="align",
    )(held(band_start), held(band_width), held(band_blocks))
    weights = pltpu.with_memory_space_constraint(weights, pltpu.VMEM)
    rowsum = pl.pallas_call(
        row_sums,
        out_shape=jax.ShapeDtypeStruct((1, rows), F32),
        in_specs=[vmem],
        out_specs=vmem,
        compiler_params=pltpu.CompilerParams(vmem_limit_bytes=8 * 1024 * 1024),
        name="row_sums",
    )(weights)
    return pl.pallas_call(
        kernel,
        out_shape=(jax.ShapeDtypeStruct((count, rows), F32), jax.ShapeDtypeStruct((count, count), F32)),
        in_specs=[hbm, hbm, vmem, vmem],
        out_specs=(vmem, vmem),
        scratch_shapes=[
            pltpu.VMEM((1, rows), F32),
            pltpu.VMEM((1, rows), F32),
            pltpu.VMEM((2, 6, count, rows), F32),
            pltpu.VMEM((window, count, rows), BF16),
            pltpu.VMEM((count, 8 * count), BF16),
            pltpu.VMEM((count, rows), F32),
            pltpu.VMEM((count, rows), F32),
            pltpu.VMEM((3 * len(PHASES), most, 8, LANE), F32),
            pltpu.SemaphoreType.DMA((6,)),
            pltpu.SemaphoreType.DMA((2, 6)),
            pltpu.SemaphoreType.DMA((3,)),
            pltpu.SemaphoreType.DMA((3,)),
            pltpu.SemaphoreType.DMA((3 * len(PHASES),)),
            pltpu.SemaphoreType.DMA((3 * len(PHASES),)),
            pltpu.SemaphoreType.DMA((2,)),
        ],
        compiler_params=pltpu.CompilerParams(
            collective_id=0, has_side_effects=True, vmem_limit_bytes=12 * 1024 * 1024
        ),
        name="subspace",
    )(held(start_vectors), held(stay), rowsum, weights)


def solution(mesh):
    placed = (
        P(None, ("grp", "st")),
        P(("grp", "st")),
        P(("grp", "st"), None),
        P(("grp", "st")),
        P(("grp", "st")),
    )
    return jax.shard_map(
        shards, mesh=mesh, in_specs=placed, out_specs=(P(None, ("grp", "st")), P()), check_vma=False
    )
```

```python
import math

import jax
import jax.numpy as jnp
from jax import lax
from jax.experimental import pallas as pl
from jax.experimental.pallas import tpu as pltpu
from jax.sharding import PartitionSpec as P

ITERS = 12
MESH = pl.DeviceIdType.MESH
F32 = jnp.float32
BF16 = jnp.bfloat16
LANE = 128
SIZES = {"yh": 2, "core": 2, "z": 4, "yl": 2, "x": 4}
PHASES = (("yh", "yl", "x"), ("core", "z"))


def split3(value):
    high = value.astype(BF16)
    rest = value - high.astype(F32)
    mid = rest.astype(BF16)
    low = (rest - mid.astype(F32)).astype(BF16)
    return high, mid, low


def coordinates():
    grp, st = lax.axis_index("grp"), lax.axis_index("st")
    return {"yh": grp // 2, "core": grp % 2, "z": st // 8, "yl": (st // 4) % 2, "x": st % 4}


def device_of(at):
    return (at["yh"] * 2 + at["core"], at["z"] * 8 + at["yl"] * 4 + at["x"])


def group(at, names):
    place = 0
    for name in names:
        place = place * SIZES[name] + at[name]
    count = 1
    for name in names:
        count *= SIZES[name]
    others = []
    for code in range(1, count):
        peer, rest = dict(at), code
        for name in reversed(names):
            step = rest % SIZES[name]
            rest //= SIZES[name]
            if step:
                peer[name] = (at[name] + step) % SIZES[name]
        others.append(device_of(peer))
    return place, count, others


def tree_sum(items):
    items = list(items)
    while len(items) > 1:
        items = [a + b for a, b in zip(items[::2], items[1::2])] + ([items[-1]] if len(items) % 2 else [])
    return items[0]


def inverse_factor(gram_rows):
    shape = (8, LANE)
    row8 = lax.broadcasted_iota(jnp.int32, shape, 0)
    lane = lax.broadcasted_iota(jnp.int32, shape, 1)
    g = list(gram_rows)
    inv = [jnp.where(lane % 32 == row8 + 8 * q, F32(1), F32(0)) for q in range(4)]
    out = []
    for p in range(4):
        cols = [[jnp.broadcast_to(g[q][:, 8 * p + k : 8 * p + k + 1], shape) for q in range(p, 4)] for k in range(8)]
        diag = jnp.ones(shape, F32)
        for j in range(8):
            pivot = jnp.broadcast_to(cols[j][0][j : j + 1, :], shape)
            diag = jnp.where(row8 == j, pivot, diag)
            scale = 1.0 / pivot
            factors = [col * scale for col in cols[j]]
            factors[0] = jnp.where(row8 > j, factors[0], F32(0))
            for k in range(j + 1, 8):
                head = jnp.broadcast_to(cols[k][0][j : j + 1, :], shape)
                cols[k] = [col - factor * head for col, factor in zip(cols[k], factors)]
            row_g = jnp.broadcast_to(g[p][j : j + 1, :], shape)
            row_i = jnp.broadcast_to(inv[p][j : j + 1, :], shape)
            for q in range(p, 4):
                if q == p and j == 7:
                    continue
                if q > p or p < 3:
                    g[q] = g[q] - factors[q - p] * row_g
                inv[q] = inv[q] - factors[q - p] * row_i
        out.append(inv[p] * (1.0 / jnp.sqrt(diag)))
    return jnp.concatenate(out, axis=0)


def align(start_ref, width_ref, band_ref, weights, raw, starts, widths, sem, small_sem):
    blocks, block_rows = raw.shape[0], raw.shape[1]
    window, rows = weights.shape
    chain = lax.axis_index("grp") * lax.axis_size("st") + lax.axis_index("st")
    ahead, pieces = 2, 2
    part = block_rows // pieces
    loads = [
        pltpu.make_async_copy(
            band_ref.at[pl.ds(k * part, part), :], raw.at[k // pieces, pl.ds((k % pieces) * part, part)], sem.at[k]
        )
        for k in range(blocks * pieces)
    ]
    for load in loads[:ahead]:
        load.start()
    small = [
        pltpu.make_async_copy(start_ref, starts, small_sem.at[0]),
        pltpu.make_async_copy(width_ref, widths, small_sem.at[1]),
    ]
    for copy in small:
        copy.start()
    for copy in small:
        copy.wait()
    for b in range(blocks):
        here = slice(b * block_rows, (b + 1) * block_rows)
        for k in range(b * pieces, (b + 1) * pieces):
            loads[k].wait()
            if k + ahead < len(loads):
                loads[k + ahead].start()
        first = (starts[b] - chain * rows) // LANE + (window - rows) // (2 * LANE)
        used = widths[b] // LANE

        def clear(e, carry, here=here):
            weights[pl.ds(pl.multiple_of(e * LANE, LANE), LANE), here] = jnp.zeros((LANE, block_rows), BF16)
            return carry

        def turn(e, carry, b=b, here=here, first=first):
            piece = raw[b, :, pl.ds(pl.multiple_of(e * LANE, LANE), LANE)]
            weights[pl.ds(pl.multiple_of((first + e) * LANE, LANE), LANE), here] = jnp.transpose(piece)
            return carry

        lax.fori_loop(0, raw.shape[2] // LANE, turn, 0, unroll=8)
        lax.fori_loop(0, first, clear, 0)
        lax.fori_loop(first + used, window // LANE, clear, 0)


def row_sums(weights, sums_ref):
    rows = sums_ref.shape[1]
    ones = jnp.ones((16, rows), BF16)
    total = jnp.zeros((8, rows), F32)
    for d in range(weights.shape[0] // rows):
        total += jnp.dot(ones, weights[d * rows : (d + 1) * rows, :], preferred_element_type=F32)[0:8]
    sums_ref[...] = total[0:1]


def kernel(
    start_ref, stay_in, rowsum_ref, weights,
    out_ref, ritz_ref,
    stay_ref, scale_ref, images, xbuf, left_ref, current, acc,
    sums,
    bulk_send, bulk_recv, row_send, row_recv, sum_send, sum_recv, input_sem,
):
    count, rows = start_ref.shape
    reach = weights.shape[0] // (2 * rows)
    devices = lax.axis_size("grp") * lax.axis_size("st")
    members = lax.axis_size("st")
    chain = lax.axis_index("grp") * members + lax.axis_index("st")
    at = coordinates()
    groups = [group(at, names) for names in PHASES]

    inputs = [
        pltpu.make_async_copy(start_ref, images.at[0, 0], input_sem.at[0]),
        pltpu.make_async_copy(stay_in, stay_ref, input_sem.at[1]),
    ]
    for copy in inputs:
        copy.start()

    x = at["x"]

    def chained(by):
        there = lax.rem(chain + by + devices, devices)
        return (there // members, there % members)

    right = device_of({**at, "x": (x + 1) % 4})
    left = device_of({**at, "x": (x + 3) % 4})
    following, preceding = chained(4), chained(-4)
    across = device_of({**at, "x": (x + 2) % 4})
    neighbours = (right, left, across, following, preceding)

    barrier = pltpu.get_barrier_semaphore()
    for device in neighbours:
        pl.semaphore_signal(barrier, inc=1, device_id=device, device_id_type=MESH)
    for device in [device for _, _, others in groups for device in others]:
        pl.semaphore_signal(barrier, inc=1, device_id=device, device_id_type=MESH)

    def pick(condition, first, second):
        return jnp.where(condition, reach + first, reach + second)

    slots = (
        reach,
        pick(x == 0, 3, -1),
        pick(x < 3, 1, -3),
        pick(x < 2, 2, -2),
        reach - 4,
        reach + 4,
        pick(x == 0, -1, 3),
        pick(x == 3, 1, -3),
        pick(x < 2, -2, 2),
    )
    half = count // 2

    def remote(src, dst, send_sem, recv_sem, device):
        return pltpu.make_async_remote_copy(
            src_ref=src, dst_ref=dst, send_sem=send_sem, recv_sem=recv_sem, device_id=device, device_id_type=MESH
        )

    def spread(parity):
        return [
            remote(images.at[parity, 0], images.at[parity, to], bulk_send.at[k], bulk_recv.at[parity, k], device)
            for k, to, device in ((0, 4, following), (1, 5, preceding), (2, 1, right), (3, 2, left))
        ]

    def onward(parity):
        return [
            remote(
                images.at[parity, src, pl.ds(first, half)],
                images.at[parity, 3, pl.ds(first, half)],
                bulk_send.at[k],
                bulk_recv.at[parity, k],
                device,
            )
            for k, src, first, device in ((4, 1, 0, right), (5, 2, half, left))
        ]

    def arrived(parity, k, block, part=None):
        ref = images.at[parity, block] if part is None else images.at[parity, block, part]
        pltpu.make_async_copy(ref, ref, bulk_recv.at[parity, k]).wait()

    before, after = 4, 5
    along = [
        remote(
            xbuf.at[jnp.where(x >= 2, before, after), pl.ds(half, half)],
            xbuf.at[8, pl.ds(half, half)],
            row_send.at[2],
            row_recv.at[2],
            across,
        ),
        remote(xbuf.at[jnp.where(x == 3, before, after)], xbuf.at[6], row_send.at[0], row_recv.at[0], right),
        remote(xbuf.at[jnp.where(x >= 1, before, after)], xbuf.at[7], row_send.at[1], row_recv.at[1], left),
    ]
    same_x = tuple(jnp.where(x < 2, a, b) for a, b in zip(following, preceding))
    over = remote(
        xbuf.at[3, pl.ds(0, half)], xbuf.at[8, pl.ds(0, half)], row_send.at[3], row_recv.at[3], same_x
    )

    def row_arrived(k, block, part=None):
        ref = xbuf.at[block] if part is None else xbuf.at[block, part]
        pltpu.make_async_copy(ref, ref, row_recv.at[k]).wait()

    row8 = lax.broadcasted_iota(jnp.int32, (count, 8 * count), 0)
    lane8 = lax.broadcasted_iota(jnp.int32, (count, 8 * count), 1)
    kept = jnp.logical_or(lane8 // 32 < 2, lane8 // 32 == 4)
    left_ref[...] = jnp.where(jnp.logical_and(kept, lane8 % 32 == row8), F32(1), F32(0)).astype(BF16)
    pl.semaphore_wait(barrier, len(neighbours) + sum(len(others) for _, _, others in groups))
    for copy in inputs:
        copy.wait()
    for copy in spread(0):
        copy.start()
    scale_ref[...] = (1.0 - stay_ref[...]) / rowsum_ref[...]
    arrived(0, 2, 1)
    arrived(0, 3, 2)
    for copy in onward(0):
        copy.start()

    def stored(slot):
        return weights[pl.ds(pl.multiple_of(slot * rows, rows), rows), :]

    def product(block):
        there = chain + (slots[block] - reach)
        valid = jnp.where(jnp.logical_and(there >= 0, there < devices), F32(1), F32(0)).astype(BF16)
        return jnp.dot(xbuf[block] * valid, stored(slots[block]), preferred_element_type=F32)

    def orthonormal(image):
        ih, im, il = split3(image)
        right = jnp.concatenate([ih, im, ih, im, il, ih, il, im], axis=0)
        return jnp.dot(left_ref[...], right, preferred_element_type=F32)

    lane8 = lax.broadcasted_iota(jnp.int32, (8, LANE), 1) // 32
    lane32 = lax.broadcasted_iota(jnp.int32, (count, LANE), 1) // 32

    def packed_product(left3, right3):
        left = jnp.concatenate(left3, axis=0)
        right = jnp.concatenate([piece for piece in right3 for _ in range(4)], axis=0)
        terms = lax.dot_general(left, right, (((1,), (1,)), ((), ())), preferred_element_type=F32)
        full = tree_sum(terms[32 * a : 32 * a + 32, LANE * b : LANE * b + LANE] for a in (2, 1, 0) for b in (2, 1, 0))
        tile = full[0:8]
        for q in range(1, 4):
            tile = jnp.where(lane8 == q, full[8 * q : 8 * q + 8], tile)
        return tile * (1.0 / (rows * devices))

    def unpacked(tile):
        return [tile] + [pltpu.roll(tile, LANE - 32 * q, 1) for q in range(1, 4)]

    stages = len(groups)
    cross = 2 * stages

    def send_all(stage, base, tile):
        place, _, others = groups[stage]
        own_slot = sums.at[base + stage, place]
        own_slot[...] = tile
        for device in others:
            pltpu.make_async_remote_copy(
                src_ref=own_slot,
                dst_ref=own_slot,
                send_sem=sum_send.at[base + stage],
                recv_sem=sum_recv.at[base + stage],
                device_id=device,
                device_id_type=MESH,
            ).start()

    def wait_all(stage, base, sem):
        part = sums.at[base + stage, pl.ds(0, len(groups[stage][2]))]
        pltpu.make_async_copy(part, part, sem.at[base + stage]).wait()

    def received(stage, base):
        wait_all(stage, base, sum_recv)
        return tree_sum(sums[base + stage, i] for i in range(groups[stage][1]))

    def one_step(t, carry):
        parity = t % 2
        final = t == ITERS - 1
        arrived(parity, 0, 4)
        xbuf[4] = orthonormal(images[parity, 4]).astype(BF16)
        arrived(parity, 1, 5)
        xbuf[5] = orthonormal(images[parity, 5]).astype(BF16)
        for copy in along:
            copy.start()
        updated = orthonormal(images[parity, 0])
        current[...] = updated
        xbuf[0] = updated.astype(BF16)
        acc[...] = product(0) + product(4) + product(5)
        arrived(parity, 4, 3, pl.ds(0, half))
        arrived(parity, 5, 3, pl.ds(half, half))
        xbuf[3] = orthonormal(images[parity, 3]).astype(BF16)
        over.start()
        xbuf[1] = orthonormal(images[parity, 1]).astype(BF16)
        xbuf[2] = orthonormal(images[parity, 2]).astype(BF16)
        acc[...] += product(1) + product(2) + product(3)
        row_arrived(0, 6)
        row_arrived(1, 7)
        acc[...] += product(6) + product(7)
        row_arrived(2, 8, pl.ds(half, half))
        row_arrived(3, 8, pl.ds(0, half))
        acc[...] += product(8)
        for copy in spread(parity) + onward(parity) + along + [over]:
            copy.wait_send()

        image = stay_ref[...] * current[...] + scale_ref[...] * acc[...]
        images[1 - parity, 0] = image
        pieces = split3(image)
        base = parity * stages
        early = spread(1 - parity)

        send_all(0, base, packed_product(pieces, pieces))

        @pl.when(jnp.logical_not(final))
        def _():
            for copy in early:
                copy.start()

        @pl.when(final)
        def _():
            send_all(0, cross, packed_product(split3(current[...]), pieces))

        for stage in range(1, stages):
            send_all(stage, base, received(stage - 1, base))

            @pl.when(final)
            def _(stage=stage):
                send_all(stage, cross, received(stage - 1, cross))

        gram = unpacked(received(stages - 1, base))

        @pl.when(jnp.logical_not(final))
        def _():
            arrived(1 - parity, 2, 1)
            arrived(1 - parity, 3, 2)
            for copy in onward(1 - parity):
                copy.start()

        for stage in range(stages):
            wait_all(stage, base, sum_send)

        high, mid, low = (piece.astype(F32) for piece in split3(inverse_factor(gram)))
        left_a = jnp.where(lane32 < 2, high, mid)
        left_b = jnp.where(lane32 == 0, high, jnp.where(lane32 == 2, mid, low))
        left_ref[...] = jnp.concatenate([left_a, left_b], axis=1).astype(BF16)
        return carry

    lax.fori_loop(0, ITERS, one_step, 0)

    out_ref[...] = orthonormal(images[ITERS % 2, 0])
    ritz = unpacked(received(stages - 1, cross))
    for q in range(4):
        ritz_ref[8 * q : 8 * q + 8, :] = ritz[q][:, 0:32]
    for stage in range(stages):
        wait_all(stage, cross, sum_send)


def shards(start_vectors, stay, band_blocks, band_start, band_width):
    count, rows = start_vectors.shape
    span = band_blocks.shape[1]
    blocks = band_start.shape[0]
    reach = span // (2 * rows)
    window = 2 * reach + 1
    vmem = pl.BlockSpec(memory_space=pltpu.VMEM)
    most = max(math.prod(SIZES[name] for name in names) for names in PHASES)
    stay = stay.reshape(1, rows)
    hbm = pl.BlockSpec(memory_space=pl.ANY)

    def held(array):
        return pltpu.with_memory_space_constraint(array, pltpu.HBM)

    weights = pl.pallas_call(
        align,
        out_shape=pltpu.VMEM((window * rows, rows), BF16),
        in_specs=[hbm, hbm, hbm],
        out_specs=vmem,
        scratch_shapes=[
            pltpu.VMEM((blocks, rows // blocks, span), BF16),
            pltpu.SMEM((blocks,), jnp.int32),
            pltpu.SMEM((blocks,), jnp.int32),
            pltpu.SemaphoreType.DMA((2 * blocks,)),
            pltpu.SemaphoreType.DMA((2,)),
        ],
        compiler_params=pltpu.CompilerParams(vmem_limit_bytes=24 * 1024 * 1024),
        name="align",
    )(held(band_start), held(band_width), held(band_blocks))
    weights = pltpu.with_memory_space_constraint(weights, pltpu.VMEM)
    rowsum = pl.pallas_call(
        row_sums,
        out_shape=jax.ShapeDtypeStruct((1, rows), F32),
        in_specs=[vmem],
        out_specs=vmem,
        compiler_params=pltpu.CompilerParams(vmem_limit_bytes=8 * 1024 * 1024),
        name="row_sums",
    )(weights)
    return pl.pallas_call(
        kernel,
        out_shape=(jax.ShapeDtypeStruct((count, rows), F32), jax.ShapeDtypeStruct((count, count), F32)),
        in_specs=[hbm, hbm, vmem, vmem],
        out_specs=(vmem, vmem),
        scratch_shapes=[
            pltpu.VMEM((1, rows), F32),
            pltpu.VMEM((1, rows), F32),
            pltpu.VMEM((2, 6, count, rows), F32),
            pltpu.VMEM((window, count, rows), BF16),
            pltpu.VMEM((count, 8 * count), BF16),
            pltpu.VMEM((count, rows), F32),
            pltpu.VMEM((count, rows), F32),
            pltpu.VMEM((3 * len(PHASES), most, 8, LANE), F32),
            pltpu.SemaphoreType.DMA((6,)),
            pltpu.SemaphoreType.DMA((2, 6)),
            pltpu.SemaphoreType.DMA((4,)),
            pltpu.SemaphoreType.DMA((4,)),
            pltpu.SemaphoreType.DMA((3 * len(PHASES),)),
            pltpu.SemaphoreType.DMA((3 * len(PHASES),)),
            pltpu.SemaphoreType.DMA((2,)),
        ],
        compiler_params=pltpu.CompilerParams(
            collective_id=0, has_side_effects=True, vmem_limit_bytes=12 * 1024 * 1024
        ),
        name="subspace",
    )(held(start_vectors), held(stay), rowsum, weights)


def solution(mesh):
    placed = (
        P(None, ("grp", "st")),
        P(("grp", "st")),
        P(("grp", "st"), None),
        P(("grp", "st")),
        P(("grp", "st")),
    )
    return jax.shard_map(
        shards, mesh=mesh, in_specs=placed, out_specs=(P(None, ("grp", "st")), P()), check_vma=False
    )
```

```python
import math

import jax
import jax.numpy as jnp
from jax import lax
from jax.experimental import pallas as pl
from jax.experimental.pallas import tpu as pltpu
from jax.sharding import PartitionSpec as P

ITERS = 12
MESH = pl.DeviceIdType.MESH
F32 = jnp.float32
BF16 = jnp.bfloat16
LANE = 128
SIZES = {"yh": 2, "core": 2, "z": 4, "yl": 2, "x": 4}
PHASES = (("yh", "yl", "x"), ("core", "z"))


def split3(value):
    high = value.astype(BF16)
    rest = value - high.astype(F32)
    mid = rest.astype(BF16)
    low = (rest - mid.astype(F32)).astype(BF16)
    return high, mid, low


def coordinates():
    grp, st = lax.axis_index("grp"), lax.axis_index("st")
    return {"yh": grp // 2, "core": grp % 2, "z": st // 8, "yl": (st // 4) % 2, "x": st % 4}


def device_of(at):
    return (at["yh"] * 2 + at["core"], at["z"] * 8 + at["yl"] * 4 + at["x"])


def group(at, names):
    place = 0
    for name in names:
        place = place * SIZES[name] + at[name]
    count = 1
    for name in names:
        count *= SIZES[name]
    others = []
    for code in range(1, count):
        peer, rest = dict(at), code
        for name in reversed(names):
            step = rest % SIZES[name]
            rest //= SIZES[name]
            if step:
                peer[name] = (at[name] + step) % SIZES[name]
        others.append(device_of(peer))
    return place, count, others


def tree_sum(items):
    items = list(items)
    while len(items) > 1:
        items = [a + b for a, b in zip(items[::2], items[1::2])] + ([items[-1]] if len(items) % 2 else [])
    return items[0]


def inverse_factor(gram_rows):
    shape = (8, LANE)
    row8 = lax.broadcasted_iota(jnp.int32, shape, 0)
    lane = lax.broadcasted_iota(jnp.int32, shape, 1)
    g = list(gram_rows)
    inv = [jnp.where(lane % 32 == row8 + 8 * q, F32(1), F32(0)) for q in range(4)]
    out = []
    for p in range(4):
        cols = [[jnp.broadcast_to(g[q][:, 8 * p + k : 8 * p + k + 1], shape) for q in range(p, 4)] for k in range(8)]
        diag = jnp.ones(shape, F32)
        for j in range(8):
            pivot = jnp.broadcast_to(cols[j][0][j : j + 1, :], shape)
            diag = jnp.where(row8 == j, pivot, diag)
            scale = 1.0 / pivot
            factors = [col * scale for col in cols[j]]
            factors[0] = jnp.where(row8 > j, factors[0], F32(0))
            for k in range(j + 1, 8):
                head = jnp.broadcast_to(cols[k][0][j : j + 1, :], shape)
                cols[k] = [col - factor * head for col, factor in zip(cols[k], factors)]
            row_g = jnp.broadcast_to(g[p][j : j + 1, :], shape)
            row_i = jnp.broadcast_to(inv[p][j : j + 1, :], shape)
            for q in range(p, 4):
                if q == p and j == 7:
                    continue
                if q > p or p < 3:
                    g[q] = g[q] - factors[q - p] * row_g
                inv[q] = inv[q] - factors[q - p] * row_i
        out.append(inv[p] * (1.0 / jnp.sqrt(diag)))
    return jnp.concatenate(out, axis=0)


def align(start_ref, width_ref, band_ref, weights, raw, starts, widths, sem, small_sem):
    blocks, block_rows = raw.shape[0], raw.shape[1]
    window, rows = weights.shape
    chain = lax.axis_index("grp") * lax.axis_size("st") + lax.axis_index("st")
    ahead, pieces = 2, 2
    part = block_rows // pieces
    loads = [
        pltpu.make_async_copy(
            band_ref.at[pl.ds(k * part, part), :], raw.at[k // pieces, pl.ds((k % pieces) * part, part)], sem.at[k]
        )
        for k in range(blocks * pieces)
    ]
    for load in loads[:ahead]:
        load.start()
    small = [
        pltpu.make_async_copy(start_ref, starts, small_sem.at[0]),
        pltpu.make_async_copy(width_ref, widths, small_sem.at[1]),
    ]
    for copy in small:
        copy.start()
    for copy in small:
        copy.wait()
    for b in range(blocks):
        here = slice(b * block_rows, (b + 1) * block_rows)
        for k in range(b * pieces, (b + 1) * pieces):
            loads[k].wait()
            if k + ahead < len(loads):
                loads[k + ahead].start()
        first = (starts[b] - chain * rows) // LANE + (window - rows) // (2 * LANE)
        used = widths[b] // LANE

        def clear(e, carry, here=here):
            weights[pl.ds(pl.multiple_of(e * LANE, LANE), LANE), here] = jnp.zeros((LANE, block_rows), BF16)
            return carry

        def turn(e, carry, b=b, here=here, first=first):
            piece = raw[b, :, pl.ds(pl.multiple_of(e * LANE, LANE), LANE)]
            weights[pl.ds(pl.multiple_of((first + e) * LANE, LANE), LANE), here] = jnp.transpose(piece)
            return carry

        lax.fori_loop(0, raw.shape[2] // LANE, turn, 0, unroll=8)
        lax.fori_loop(0, first, clear, 0)
        lax.fori_loop(first + used, window // LANE, clear, 0)


def row_scale(stay_ref, weights, scale_ref):
    rows = stay_ref.shape[1]
    ones = jnp.ones((16, rows), BF16)
    total = jnp.zeros((8, rows), F32)
    for d in range(weights.shape[0] // rows):
        total += jnp.dot(ones, weights[d * rows : (d + 1) * rows, :], preferred_element_type=F32)[0:8]
    scale_ref[...] = (1.0 - stay_ref[...]) / total[0:1]


def kernel(
    start_ref, stay_ref, scale_ref, weights,
    out_ref, ritz_ref,
    images, xbuf, left_ref, current, acc,
    sums,
    bulk_send, bulk_recv, row_send, row_recv, sum_send, sum_recv,
):
    count, rows = start_ref.shape
    reach = weights.shape[0] // (2 * rows)
    devices = lax.axis_size("grp") * lax.axis_size("st")
    members = lax.axis_size("st")
    chain = lax.axis_index("grp") * members + lax.axis_index("st")
    at = coordinates()
    groups = [group(at, names) for names in PHASES]

    x = at["x"]

    def chained(by):
        there = lax.rem(chain + by + devices, devices)
        return (there // members, there % members)

    right = device_of({**at, "x": (x + 1) % 4})
    left = device_of({**at, "x": (x + 3) % 4})
    following, preceding = chained(4), chained(-4)
    across = device_of({**at, "x": (x + 2) % 4})
    neighbours = (right, left, across, following, preceding)

    barrier = pltpu.get_barrier_semaphore()
    for device in neighbours:
        pl.semaphore_signal(barrier, inc=1, device_id=device, device_id_type=MESH)
    for device in [device for _, _, others in groups for device in others]:
        pl.semaphore_signal(barrier, inc=1, device_id=device, device_id_type=MESH)

    def pick(condition, first, second):
        return jnp.where(condition, reach + first, reach + second)

    slots = (
        reach,
        pick(x == 0, 3, -1),
        pick(x < 3, 1, -3),
        pick(x < 2, 2, -2),
        reach - 4,
        reach + 4,
        pick(x == 0, -1, 3),
        pick(x == 3, 1, -3),
        pick(x < 2, -2, 2),
    )
    half = count // 2

    def remote(src, dst, send_sem, recv_sem, device):
        return pltpu.make_async_remote_copy(
            src_ref=src, dst_ref=dst, send_sem=send_sem, recv_sem=recv_sem, device_id=device, device_id_type=MESH
        )

    def spread(parity):
        return [
            remote(images.at[parity, 0], images.at[parity, to], bulk_send.at[k], bulk_recv.at[parity, k], device)
            for k, to, device in ((0, 4, following), (1, 5, preceding), (2, 1, right), (3, 2, left))
        ]

    def onward(parity):
        return [
            remote(
                images.at[parity, src, pl.ds(first, half)],
                images.at[parity, 3, pl.ds(first, half)],
                bulk_send.at[k],
                bulk_recv.at[parity, k],
                device,
            )
            for k, src, first, device in ((4, 1, 0, right), (5, 2, half, left))
        ]

    def arrived(parity, k, block, part=None):
        ref = images.at[parity, block] if part is None else images.at[parity, block, part]
        pltpu.make_async_copy(ref, ref, bulk_recv.at[parity, k]).wait()

    before, after = 4, 5
    along = [
        remote(xbuf.at[jnp.where(x >= 2, before, after)], xbuf.at[8], row_send.at[2], row_recv.at[2], across),
        remote(xbuf.at[jnp.where(x == 3, before, after)], xbuf.at[6], row_send.at[0], row_recv.at[0], right),
        remote(xbuf.at[jnp.where(x >= 1, before, after)], xbuf.at[7], row_send.at[1], row_recv.at[1], left),
    ]

    images[0, 0] = start_ref[...]
    row8 = lax.broadcasted_iota(jnp.int32, (count, 8 * count), 0)
    lane8 = lax.broadcasted_iota(jnp.int32, (count, 8 * count), 1)
    kept = jnp.logical_or(lane8 // 32 < 2, lane8 // 32 == 4)
    left_ref[...] = jnp.where(jnp.logical_and(kept, lane8 % 32 == row8), F32(1), F32(0)).astype(BF16)
    pl.semaphore_wait(barrier, len(neighbours) + sum(len(others) for _, _, others in groups))
    for copy in spread(0):
        copy.start()
    arrived(0, 2, 1)
    arrived(0, 3, 2)
    for copy in onward(0):
        copy.start()

    def stored(slot):
        return weights[pl.ds(pl.multiple_of(slot * rows, rows), rows), :]

    def product(block):
        there = chain + (slots[block] - reach)
        valid = jnp.where(jnp.logical_and(there >= 0, there < devices), F32(1), F32(0)).astype(BF16)
        return jnp.dot(xbuf[block] * valid, stored(slots[block]), preferred_element_type=F32)

    def orthonormal(image):
        ih, im, il = split3(image)
        right = jnp.concatenate([ih, im, ih, im, il, ih, il, im], axis=0)
        return jnp.dot(left_ref[...], right, preferred_element_type=F32)

    lane8 = lax.broadcasted_iota(jnp.int32, (8, LANE), 1) // 32
    lane32 = lax.broadcasted_iota(jnp.int32, (count, LANE), 1) // 32

    def packed_product(left3, right3):
        left = jnp.concatenate(left3, axis=0)
        right = jnp.concatenate([piece for piece in right3 for _ in range(4)], axis=0)
        terms = lax.dot_general(left, right, (((1,), (1,)), ((), ())), preferred_element_type=F32)
        full = tree_sum(terms[32 * a : 32 * a + 32, LANE * b : LANE * b + LANE] for a in (2, 1, 0) for b in (2, 1, 0))
        tile = full[0:8]
        for q in range(1, 4):
            tile = jnp.where(lane8 == q, full[8 * q : 8 * q + 8], tile)
        return tile * (1.0 / (rows * devices))

    def unpacked(tile):
        return [tile] + [pltpu.roll(tile, LANE - 32 * q, 1) for q in range(1, 4)]

    stages = len(groups)
    cross = 2 * stages

    def send_all(stage, base, tile):
        place, _, others = groups[stage]
        own_slot = sums.at[base + stage, place]
        own_slot[...] = tile
        for device in others:
            pltpu.make_async_remote_copy(
                src_ref=own_slot,
                dst_ref=own_slot,
                send_sem=sum_send.at[base + stage],
                recv_sem=sum_recv.at[base + stage],
                device_id=device,
                device_id_type=MESH,
            ).start()

    def wait_all(stage, base, sem):
        part = sums.at[base + stage, pl.ds(0, len(groups[stage][2]))]
        pltpu.make_async_copy(part, part, sem.at[base + stage]).wait()

    def received(stage, base):
        wait_all(stage, base, sum_recv)
        return tree_sum(sums[base + stage, i] for i in range(groups[stage][1]))

    def one_step(t, carry):
        parity = t % 2
        final = t == ITERS - 1
        arrived(parity, 0, 4)
        xbuf[4] = orthonormal(images[parity, 4]).astype(BF16)
        arrived(parity, 1, 5)
        xbuf[5] = orthonormal(images[parity, 5]).astype(BF16)
        for copy in along:
            copy.start()
        updated = orthonormal(images[parity, 0])
        current[...] = updated
        xbuf[0] = updated.astype(BF16)
        acc[...] = product(0) + product(4) + product(5)
        xbuf[1] = orthonormal(images[parity, 1]).astype(BF16)
        xbuf[2] = orthonormal(images[parity, 2]).astype(BF16)
        acc[...] += product(1) + product(2)
        arrived(parity, 4, 3, pl.ds(0, half))
        arrived(parity, 5, 3, pl.ds(half, half))
        xbuf[3] = orthonormal(images[parity, 3]).astype(BF16)
        acc[...] += product(3)
        for k, block in ((0, 6), (1, 7), (2, 8)):
            pltpu.make_async_copy(xbuf.at[block], xbuf.at[block], row_recv.at[k]).wait()
        acc[...] += product(6) + product(7) + product(8)
        image = stay_ref[...] * current[...] + scale_ref[...] * acc[...]
        images[1 - parity, 0] = image
        pieces = split3(image)
        base = parity * stages
        tile = packed_product(pieces, pieces)
        for copy in spread(parity) + onward(parity) + along:
            copy.wait_send()
        send_all(0, base, tile)

        @pl.when(jnp.logical_not(final))
        def _():
            for copy in spread(1 - parity):
                copy.start()

        @pl.when(final)
        def _():
            send_all(0, cross, packed_product(split3(current[...]), pieces))

        for stage in range(1, stages):
            send_all(stage, base, received(stage - 1, base))

            @pl.when(final)
            def _(stage=stage):
                send_all(stage, cross, received(stage - 1, cross))

        @pl.when(jnp.logical_not(final))
        def _():
            arrived(1 - parity, 2, 1)
            arrived(1 - parity, 3, 2)
            for copy in onward(1 - parity):
                copy.start()

        gram = unpacked(received(stages - 1, base))
        high, mid, low = (piece.astype(F32) for piece in split3(inverse_factor(gram)))
        left_a = jnp.where(lane32 < 2, high, mid)
        left_b = jnp.where(lane32 == 0, high, jnp.where(lane32 == 2, mid, low))
        left_ref[...] = jnp.concatenate([left_a, left_b], axis=1).astype(BF16)
        for stage in range(stages):
            wait_all(stage, base, sum_send)
        return carry

    lax.fori_loop(0, ITERS, one_step, 0)

    out_ref[...] = orthonormal(images[ITERS % 2, 0])
    ritz = unpacked(received(stages - 1, cross))
    for q in range(4):
        ritz_ref[8 * q : 8 * q + 8, :] = ritz[q][:, 0:32]
    for stage in range(stages):
        wait_all(stage, cross, sum_send)


def shards(start_vectors, stay, band_blocks, band_start, band_width):
    count, rows = start_vectors.shape
    span = band_blocks.shape[1]
    blocks = band_start.shape[0]
    reach = span // (2 * rows)
    window = 2 * reach + 1
    vmem = pl.BlockSpec(memory_space=pltpu.VMEM)
    most = max(math.prod(SIZES[name] for name in names) for names in PHASES)
    stay = stay.reshape(1, rows)
    hbm = pl.BlockSpec(memory_space=pl.ANY)

    def held(array):
        return pltpu.with_memory_space_constraint(array, pltpu.HBM)

    weights = pl.pallas_call(
        align,
        out_shape=pltpu.VMEM((window * rows, rows), BF16),
        in_specs=[hbm, hbm, hbm],
        out_specs=vmem,
        scratch_shapes=[
            pltpu.VMEM((blocks, rows // blocks, span), BF16),
            pltpu.SMEM((blocks,), jnp.int32),
            pltpu.SMEM((blocks,), jnp.int32),
            pltpu.SemaphoreType.DMA((2 * blocks,)),
            pltpu.SemaphoreType.DMA((2,)),
        ],
        compiler_params=pltpu.CompilerParams(vmem_limit_bytes=24 * 1024 * 1024),
        name="align",
    )(held(band_start), held(band_width), held(band_blocks))
    weights = pltpu.with_memory_space_constraint(weights, pltpu.VMEM)
    scale = pl.pallas_call(
        row_scale,
        out_shape=jax.ShapeDtypeStruct((1, rows), F32),
        in_specs=[vmem, vmem],
        out_specs=vmem,
        compiler_params=pltpu.CompilerParams(vmem_limit_bytes=8 * 1024 * 1024),
        name="row_scale",
    )(stay, weights)
    return pl.pallas_call(
        kernel,
        out_shape=(jax.ShapeDtypeStruct((count, rows), F32), jax.ShapeDtypeStruct((count, count), F32)),
        in_specs=[vmem, vmem, vmem, vmem],
        out_specs=(vmem, vmem),
        scratch_shapes=[
            pltpu.VMEM((2, 6, count, rows), F32),
            pltpu.VMEM((window, count, rows), BF16),
            pltpu.VMEM((count, 8 * count), BF16),
            pltpu.VMEM((count, rows), F32),
            pltpu.VMEM((count, rows), F32),
            pltpu.VMEM((3 * len(PHASES), most, 8, LANE), F32),
            pltpu.SemaphoreType.DMA((6,)),
            pltpu.SemaphoreType.DMA((2, 6)),
            pltpu.SemaphoreType.DMA((3,)),
            pltpu.SemaphoreType.DMA((3,)),
            pltpu.SemaphoreType.DMA((3 * len(PHASES),)),
            pltpu.SemaphoreType.DMA((3 * len(PHASES),)),
        ],
        compiler_params=pltpu.CompilerParams(
            collective_id=0, has_side_effects=True, vmem_limit_bytes=12 * 1024 * 1024
        ),
        name="subspace",
    )(start_vectors, stay, scale, weights)


def solution(mesh):
    placed = (
        P(None, ("grp", "st")),
        P(("grp", "st")),
        P(("grp", "st"), None),
        P(("grp", "st")),
        P(("grp", "st")),
    )
    return jax.shard_map(
        shards, mesh=mesh, in_specs=placed, out_specs=(P(None, ("grp", "st")), P()), check_vma=False
    )
```

```python
import math

import jax
import jax.numpy as jnp
from jax import lax
from jax.experimental import pallas as pl
from jax.experimental.pallas import tpu as pltpu
from jax.sharding import PartitionSpec as P

ITERS = 12
MESH = pl.DeviceIdType.MESH
F32 = jnp.float32
BF16 = jnp.bfloat16
LANE = 128
SIZES = {"yh": 2, "core": 2, "z": 4, "yl": 2, "x": 4}
PHASES = (("yh", "yl", "x"), ("core", "z"))


def split3(value):
    high = value.astype(BF16)
    rest = value - high.astype(F32)
    mid = rest.astype(BF16)
    low = (rest - mid.astype(F32)).astype(BF16)
    return high, mid, low


def coordinates():
    grp, st = lax.axis_index("grp"), lax.axis_index("st")
    return {"yh": grp // 2, "core": grp % 2, "z": st // 8, "yl": (st // 4) % 2, "x": st % 4}


def device_of(at):
    return (at["yh"] * 2 + at["core"], at["z"] * 8 + at["yl"] * 4 + at["x"])


def group(at, names):
    place = 0
    for name in names:
        place = place * SIZES[name] + at[name]
    count = 1
    for name in names:
        count *= SIZES[name]
    others = []
    for code in range(1, count):
        peer, rest = dict(at), code
        for name in reversed(names):
            step = rest % SIZES[name]
            rest //= SIZES[name]
            if step:
                peer[name] = (at[name] + step) % SIZES[name]
        others.append(device_of(peer))
    return place, count, others


def tree_sum(items):
    items = list(items)
    while len(items) > 1:
        items = [a + b for a, b in zip(items[::2], items[1::2])] + ([items[-1]] if len(items) % 2 else [])
    return items[0]


def inverse_factor(gram_rows):
    shape = (8, LANE)
    row8 = lax.broadcasted_iota(jnp.int32, shape, 0)
    lane = lax.broadcasted_iota(jnp.int32, shape, 1)
    g = list(gram_rows)
    inv = [jnp.where(lane % 32 == row8 + 8 * q, F32(1), F32(0)) for q in range(4)]
    out = []
    for p in range(4):
        cols = [[jnp.broadcast_to(g[q][:, 8 * p + k : 8 * p + k + 1], shape) for q in range(p, 4)] for k in range(8)]
        diag = jnp.ones(shape, F32)
        for j in range(8):
            pivot = jnp.broadcast_to(cols[j][0][j : j + 1, :], shape)
            diag = jnp.where(row8 == j, pivot, diag)
            scale = 1.0 / pivot
            factors = [col * scale for col in cols[j]]
            factors[0] = jnp.where(row8 > j, factors[0], F32(0))
            for k in range(j + 1, 8):
                head = jnp.broadcast_to(cols[k][0][j : j + 1, :], shape)
                cols[k] = [col - factor * head for col, factor in zip(cols[k], factors)]
            row_g = jnp.broadcast_to(g[p][j : j + 1, :], shape)
            row_i = jnp.broadcast_to(inv[p][j : j + 1, :], shape)
            for q in range(p, 4):
                if q == p and j == 7:
                    continue
                if q > p or p < 3:
                    g[q] = g[q] - factors[q - p] * row_g
                inv[q] = inv[q] - factors[q - p] * row_i
        out.append(inv[p] * (1.0 / jnp.sqrt(diag)))
    return jnp.concatenate(out, axis=0)


def align(start_ref, width_ref, band_ref, weights, raw, starts, widths, sem, small_sem):
    blocks, block_rows = raw.shape[0], raw.shape[1]
    window, rows = weights.shape
    chain = lax.axis_index("grp") * lax.axis_size("st") + lax.axis_index("st")
    ahead, pieces = 2, 2
    part = block_rows // pieces
    loads = [
        pltpu.make_async_copy(
            band_ref.at[pl.ds(k * part, part), :], raw.at[k // pieces, pl.ds((k % pieces) * part, part)], sem.at[k]
        )
        for k in range(blocks * pieces)
    ]
    for load in loads[:ahead]:
        load.start()
    small = [
        pltpu.make_async_copy(start_ref, starts, small_sem.at[0]),
        pltpu.make_async_copy(width_ref, widths, small_sem.at[1]),
    ]
    for copy in small:
        copy.start()
    for copy in small:
        copy.wait()
    for b in range(blocks):
        here = slice(b * block_rows, (b + 1) * block_rows)
        for k in range(b * pieces, (b + 1) * pieces):
            loads[k].wait()
            if k + ahead < len(loads):
                loads[k + ahead].start()
        first = (starts[b] - chain * rows) // LANE + (window - rows) // (2 * LANE)
        used = widths[b] // LANE

        def clear(e, carry, here=here):
            weights[pl.ds(pl.multiple_of(e * LANE, LANE), LANE), here] = jnp.zeros((LANE, block_rows), BF16)
            return carry

        def turn(e, carry, b=b, here=here, first=first):
            piece = raw[b, :, pl.ds(pl.multiple_of(e * LANE, LANE), LANE)]
            weights[pl.ds(pl.multiple_of((first + e) * LANE, LANE), LANE), here] = jnp.transpose(piece)
            return carry

        lax.fori_loop(0, raw.shape[2] // LANE, turn, 0, unroll=8)
        lax.fori_loop(0, first, clear, 0)
        lax.fori_loop(first + used, window // LANE, clear, 0)


def row_scale(stay_ref, weights, scale_ref):
    rows = stay_ref.shape[1]
    ones = jnp.ones((16, rows), BF16)
    total = jnp.zeros((8, rows), F32)
    for d in range(weights.shape[0] // rows):
        total += jnp.dot(ones, weights[d * rows : (d + 1) * rows, :], preferred_element_type=F32)[0:8]
    scale_ref[...] = (1.0 - stay_ref[...]) / total[0:1]


def kernel(
    start_ref, stay_ref, scale_ref, weights,
    out_ref, ritz_ref,
    images, xbuf, left_ref, current, acc,
    sums,
    bulk_send, bulk_recv, row_send, row_recv, sum_send, sum_recv,
):
    count, rows = start_ref.shape
    reach = weights.shape[0] // (2 * rows)
    devices = lax.axis_size("grp") * lax.axis_size("st")
    members = lax.axis_size("st")
    chain = lax.axis_index("grp") * members + lax.axis_index("st")
    at = coordinates()
    groups = [group(at, names) for names in PHASES]

    x = at["x"]

    def chained(by):
        there = lax.rem(chain + by + devices, devices)
        return (there // members, there % members)

    right = device_of({**at, "x": (x + 1) % 4})
    left = device_of({**at, "x": (x + 3) % 4})
    following, preceding = chained(4), chained(-4)
    across = device_of({**at, "x": (x + 2) % 4})
    neighbours = (right, left, across, following, preceding)

    barrier = pltpu.get_barrier_semaphore()
    for device in neighbours:
        pl.semaphore_signal(barrier, inc=1, device_id=device, device_id_type=MESH)
    for device in [device for _, _, others in groups for device in others]:
        pl.semaphore_signal(barrier, inc=1, device_id=device, device_id_type=MESH)

    def pick(condition, first, second):
        return jnp.where(condition, reach + first, reach + second)

    slots = (
        reach,
        pick(x == 0, 3, -1),
        pick(x < 3, 1, -3),
        pick(x < 2, 2, -2),
        reach - 4,
        reach + 4,
        pick(x == 0, -1, 3),
        pick(x == 3, 1, -3),
        pick(x < 2, -2, 2),
    )
    half = count // 2

    def remote(src, dst, send_sem, recv_sem, device):
        return pltpu.make_async_remote_copy(
            src_ref=src, dst_ref=dst, send_sem=send_sem, recv_sem=recv_sem, device_id=device, device_id_type=MESH
        )

    def spread(parity):
        return [
            remote(images.at[parity, 0], images.at[parity, to], bulk_send.at[k], bulk_recv.at[parity, k], device)
            for k, to, device in ((2, 1, right), (3, 2, left), (0, 4, following), (1, 5, preceding))
        ]

    def onward(parity):
        return [
            remote(
                images.at[parity, src, pl.ds(first, half)],
                images.at[parity, 3, pl.ds(first, half)],
                bulk_send.at[k],
                bulk_recv.at[parity, k],
                device,
            )
            for k, src, first, device in ((4, 1, 0, right), (5, 2, half, left))
        ]

    def arrived(parity, k, block, part=None):
        ref = images.at[parity, block] if part is None else images.at[parity, block, part]
        pltpu.make_async_copy(ref, ref, bulk_recv.at[parity, k]).wait()

    before, after = 4, 5
    along = [
        remote(xbuf.at[jnp.where(x >= 2, before, after)], xbuf.at[8], row_send.at[2], row_recv.at[2], across),
        remote(xbuf.at[jnp.where(x == 3, before, after)], xbuf.at[6], row_send.at[0], row_recv.at[0], right),
        remote(xbuf.at[jnp.where(x >= 1, before, after)], xbuf.at[7], row_send.at[1], row_recv.at[1], left),
    ]

    images[0, 0] = start_ref[...]
    row8 = lax.broadcasted_iota(jnp.int32, (count, 8 * count), 0)
    lane8 = lax.broadcasted_iota(jnp.int32, (count, 8 * count), 1)
    kept = jnp.logical_or(lane8 // 32 < 2, lane8 // 32 == 4)
    left_ref[...] = jnp.where(jnp.logical_and(kept, lane8 % 32 == row8), F32(1), F32(0)).astype(BF16)
    pl.semaphore_wait(barrier, len(neighbours) + sum(len(others) for _, _, others in groups))
    for copy in spread(0):
        copy.start()
    arrived(0, 2, 1)
    arrived(0, 3, 2)
    for copy in onward(0):
        copy.start()

    def stored(slot):
        return weights[pl.ds(pl.multiple_of(slot * rows, rows), rows), :]

    def product(block):
        there = chain + (slots[block] - reach)
        valid = jnp.where(jnp.logical_and(there >= 0, there < devices), F32(1), F32(0)).astype(BF16)
        return jnp.dot(xbuf[block] * valid, stored(slots[block]), preferred_element_type=F32)

    def orthonormal(image):
        ih, im, il = split3(image)
        right = jnp.concatenate([ih, im, ih, im, il, ih, il, im], axis=0)
        return jnp.dot(left_ref[...], right, preferred_element_type=F32)

    lane8 = lax.broadcasted_iota(jnp.int32, (8, LANE), 1) // 32
    lane32 = lax.broadcasted_iota(jnp.int32, (count, LANE), 1) // 32

    def packed_product(left3, right3):
        left = jnp.concatenate(left3, axis=0)
        right = jnp.concatenate([piece for piece in right3 for _ in range(4)], axis=0)
        terms = lax.dot_general(left, right, (((1,), (1,)), ((), ())), preferred_element_type=F32)
        full = tree_sum(terms[32 * a : 32 * a + 32, LANE * b : LANE * b + LANE] for a in (2, 1, 0) for b in (2, 1, 0))
        tile = full[0:8]
        for q in range(1, 4):
            tile = jnp.where(lane8 == q, full[8 * q : 8 * q + 8], tile)
        return tile * (1.0 / (rows * devices))

    def unpacked(tile):
        return [tile] + [pltpu.roll(tile, LANE - 32 * q, 1) for q in range(1, 4)]

    stages = len(groups)
    cross = 2 * stages

    def send_all(stage, base, tile):
        place, _, others = groups[stage]
        own_slot = sums.at[base + stage, place]
        own_slot[...] = tile
        for device in others:
            pltpu.make_async_remote_copy(
                src_ref=own_slot,
                dst_ref=own_slot,
                send_sem=sum_send.at[base + stage],
                recv_sem=sum_recv.at[base + stage],
                device_id=device,
                device_id_type=MESH,
            ).start()

    def wait_all(stage, base, sem):
        part = sums.at[base + stage, pl.ds(0, len(groups[stage][2]))]
        pltpu.make_async_copy(part, part, sem.at[base + stage]).wait()

    def received(stage, base):
        wait_all(stage, base, sum_recv)
        return tree_sum(sums[base + stage, i] for i in range(groups[stage][1]))

    def one_step(t, carry):
        parity = t % 2
        final = t == ITERS - 1
        arrived(parity, 0, 4)
        xbuf[4] = orthonormal(images[parity, 4]).astype(BF16)
        arrived(parity, 1, 5)
        xbuf[5] = orthonormal(images[parity, 5]).astype(BF16)
        for copy in along:
            copy.start()
        updated = orthonormal(images[parity, 0])
        current[...] = updated
        xbuf[0] = updated.astype(BF16)
        acc[...] = product(0) + product(4) + product(5)
        xbuf[1] = orthonormal(images[parity, 1]).astype(BF16)
        xbuf[2] = orthonormal(images[parity, 2]).astype(BF16)
        acc[...] += product(1) + product(2)
        arrived(parity, 4, 3, pl.ds(0, half))
        arrived(parity, 5, 3, pl.ds(half, half))
        xbuf[3] = orthonormal(images[parity, 3]).astype(BF16)
        acc[...] += product(3)
        for k, block in ((0, 6), (1, 7), (2, 8)):
            pltpu.make_async_copy(xbuf.at[block], xbuf.at[block], row_recv.at[k]).wait()
        acc[...] += product(6) + product(7) + product(8)
        image = stay_ref[...] * current[...] + scale_ref[...] * acc[...]
        images[1 - parity, 0] = image
        pieces = split3(image)
        base = parity * stages
        tile = packed_product(pieces, pieces)
        for copy in spread(parity) + onward(parity) + along:
            copy.wait_send()
        send_all(0, base, tile)

        @pl.when(jnp.logical_not(final))
        def _():
            for copy in spread(1 - parity):
                copy.start()

        @pl.when(final)
        def _():
            send_all(0, cross, packed_product(split3(current[...]), pieces))

        for stage in range(1, stages):
            send_all(stage, base, received(stage - 1, base))

            @pl.when(final)
            def _(stage=stage):
                send_all(stage, cross, received(stage - 1, cross))

        @pl.when(jnp.logical_not(final))
        def _():
            arrived(1 - parity, 2, 1)
            arrived(1 - parity, 3, 2)
            for copy in onward(1 - parity):
                copy.start()

        gram = unpacked(received(stages - 1, base))
        high, mid, low = (piece.astype(F32) for piece in split3(inverse_factor(gram)))
        left_a = jnp.where(lane32 < 2, high, mid)
        left_b = jnp.where(lane32 == 0, high, jnp.where(lane32 == 2, mid, low))
        left_ref[...] = jnp.concatenate([left_a, left_b], axis=1).astype(BF16)
        for stage in range(stages):
            wait_all(stage, base, sum_send)
        return carry

    lax.fori_loop(0, ITERS, one_step, 0)

    out_ref[...] = orthonormal(images[ITERS % 2, 0])
    ritz = unpacked(received(stages - 1, cross))
    for q in range(4):
        ritz_ref[8 * q : 8 * q + 8, :] = ritz[q][:, 0:32]
    for stage in range(stages):
        wait_all(stage, cross, sum_send)


def shards(start_vectors, stay, band_blocks, band_start, band_width):
    count, rows = start_vectors.shape
    span = band_blocks.shape[1]
    blocks = band_start.shape[0]
    reach = span // (2 * rows)
    window = 2 * reach + 1
    vmem = pl.BlockSpec(memory_space=pltpu.VMEM)
    most = max(math.prod(SIZES[name] for name in names) for names in PHASES)
    stay = stay.reshape(1, rows)
    hbm = pl.BlockSpec(memory_space=pl.ANY)

    def held(array):
        return pltpu.with_memory_space_constraint(array, pltpu.HBM)

    weights = pl.pallas_call(
        align,
        out_shape=pltpu.VMEM((window * rows, rows), BF16),
        in_specs=[hbm, hbm, hbm],
        out_specs=vmem,
        scratch_shapes=[
            pltpu.VMEM((blocks, rows // blocks, span), BF16),
            pltpu.SMEM((blocks,), jnp.int32),
            pltpu.SMEM((blocks,), jnp.int32),
            pltpu.SemaphoreType.DMA((2 * blocks,)),
            pltpu.SemaphoreType.DMA((2,)),
        ],
        compiler_params=pltpu.CompilerParams(vmem_limit_bytes=24 * 1024 * 1024),
        name="align",
    )(held(band_start), held(band_width), held(band_blocks))
    weights = pltpu.with_memory_space_constraint(weights, pltpu.VMEM)
    scale = pl.pallas_call(
        row_scale,
        out_shape=jax.ShapeDtypeStruct((1, rows), F32),
        in_specs=[vmem, vmem],
        out_specs=vmem,
        compiler_params=pltpu.CompilerParams(vmem_limit_bytes=8 * 1024 * 1024),
        name="row_scale",
    )(stay, weights)
    return pl.pallas_call(
        kernel,
        out_shape=(jax.ShapeDtypeStruct((count, rows), F32), jax.ShapeDtypeStruct((count, count), F32)),
        in_specs=[vmem, vmem, vmem, vmem],
        out_specs=(vmem, vmem),
        scratch_shapes=[
            pltpu.VMEM((2, 6, count, rows), F32),
            pltpu.VMEM((window, count, rows), BF16),
            pltpu.VMEM((count, 8 * count), BF16),
            pltpu.VMEM((count, rows), F32),
            pltpu.VMEM((count, rows), F32),
            pltpu.VMEM((3 * len(PHASES), most, 8, LANE), F32),
            pltpu.SemaphoreType.DMA((6,)),
            pltpu.SemaphoreType.DMA((2, 6)),
            pltpu.SemaphoreType.DMA((3,)),
            pltpu.SemaphoreType.DMA((3,)),
            pltpu.SemaphoreType.DMA((3 * len(PHASES),)),
            pltpu.SemaphoreType.DMA((3 * len(PHASES),)),
        ],
        compiler_params=pltpu.CompilerParams(
            collective_id=0, has_side_effects=True, vmem_limit_bytes=12 * 1024 * 1024
        ),
        name="subspace",
    )(start_vectors, stay, scale, weights)


def solution(mesh):
    placed = (
        P(None, ("grp", "st")),
        P(("grp", "st")),
        P(("grp", "st"), None),
        P(("grp", "st")),
        P(("grp", "st")),
    )
    return jax.shard_map(
        shards, mesh=mesh, in_specs=placed, out_specs=(P(None, ("grp", "st")), P()), check_vma=False
    )
```

```python
import math

import jax
import jax.numpy as jnp
from jax import lax
from jax.experimental import pallas as pl
from jax.experimental.pallas import tpu as pltpu
from jax.sharding import PartitionSpec as P

ITERS = 12
MESH = pl.DeviceIdType.MESH
F32 = jnp.float32
BF16 = jnp.bfloat16
LANE = 128
SIZES = {"yh": 2, "core": 2, "z": 4, "yl": 2, "x": 4}
PHASES = (("yh", "yl", "x"), ("core", "z"))


def split3(value):
    high = value.astype(BF16)
    rest = value - high.astype(F32)
    mid = rest.astype(BF16)
    low = (rest - mid.astype(F32)).astype(BF16)
    return high, mid, low


def coordinates():
    grp, st = lax.axis_index("grp"), lax.axis_index("st")
    return {"yh": grp // 2, "core": grp % 2, "z": st // 8, "yl": (st // 4) % 2, "x": st % 4}


def device_of(at):
    return (at["yh"] * 2 + at["core"], at["z"] * 8 + at["yl"] * 4 + at["x"])


def group(at, names):
    place = 0
    for name in names:
        place = place * SIZES[name] + at[name]
    count = 1
    for name in names:
        count *= SIZES[name]
    others = []
    for code in range(1, count):
        peer, rest = dict(at), code
        for name in reversed(names):
            step = rest % SIZES[name]
            rest //= SIZES[name]
            if step:
                peer[name] = (at[name] + step) % SIZES[name]
        others.append(device_of(peer))
    return place, count, others


def tree_sum(items):
    items = list(items)
    while len(items) > 1:
        items = [a + b for a, b in zip(items[::2], items[1::2])] + ([items[-1]] if len(items) % 2 else [])
    return items[0]


def inverse_factor(gram_rows):
    shape = (8, LANE)
    row8 = lax.broadcasted_iota(jnp.int32, shape, 0)
    lane = lax.broadcasted_iota(jnp.int32, shape, 1)
    g = list(gram_rows)
    inv = [jnp.where(lane % 32 == row8 + 8 * q, F32(1), F32(0)) for q in range(4)]
    out = []
    for p in range(4):
        cols = [[jnp.broadcast_to(g[q][:, 8 * p + k : 8 * p + k + 1], shape) for q in range(p, 4)] for k in range(8)]
        diag = jnp.ones(shape, F32)
        for j in range(8):
            pivot = jnp.broadcast_to(cols[j][0][j : j + 1, :], shape)
            diag = jnp.where(row8 == j, pivot, diag)
            scale = 1.0 / pivot
            factors = [col * scale for col in cols[j]]
            factors[0] = jnp.where(row8 > j, factors[0], F32(0))
            for k in range(j + 1, 8):
                head = jnp.broadcast_to(cols[k][0][j : j + 1, :], shape)
                cols[k] = [col - factor * head for col, factor in zip(cols[k], factors)]
            row_g = jnp.broadcast_to(g[p][j : j + 1, :], shape)
            row_i = jnp.broadcast_to(inv[p][j : j + 1, :], shape)
            for q in range(p, 4):
                if q == p and j == 7:
                    continue
                if q > p or p < 3:
                    g[q] = g[q] - factors[q - p] * row_g
                inv[q] = inv[q] - factors[q - p] * row_i
        out.append(inv[p] * (1.0 / jnp.sqrt(diag)))
    return jnp.concatenate(out, axis=0)


def align(start_ref, width_ref, band_ref, weights, raw, starts, widths, sem, small_sem):
    blocks, block_rows = raw.shape[0], raw.shape[1]
    window, rows = weights.shape
    chain = lax.axis_index("grp") * lax.axis_size("st") + lax.axis_index("st")
    ahead, pieces = 2, 2
    part = block_rows // pieces
    loads = [
        pltpu.make_async_copy(
            band_ref.at[pl.ds(k * part, part), :], raw.at[k // pieces, pl.ds((k % pieces) * part, part)], sem.at[k]
        )
        for k in range(blocks * pieces)
    ]
    for load in loads[:ahead]:
        load.start()
    small = [
        pltpu.make_async_copy(start_ref, starts, small_sem.at[0]),
        pltpu.make_async_copy(width_ref, widths, small_sem.at[1]),
    ]
    for copy in small:
        copy.start()
    for copy in small:
        copy.wait()
    for b in range(blocks):
        here = slice(b * block_rows, (b + 1) * block_rows)
        for k in range(b * pieces, (b + 1) * pieces):
            loads[k].wait()
            if k + ahead < len(loads):
                loads[k + ahead].start()
        first = (starts[b] - chain * rows) // LANE + (window - rows) // (2 * LANE)
        used = widths[b] // LANE

        def clear(e, carry, here=here):
            weights[pl.ds(pl.multiple_of(e * LANE, LANE), LANE), here] = jnp.zeros((LANE, block_rows), BF16)
            return carry

        def turn(e, carry, b=b, here=here, first=first):
            piece = raw[b, :, pl.ds(pl.multiple_of(e * LANE, LANE), LANE)]
            weights[pl.ds(pl.multiple_of((first + e) * LANE, LANE), LANE), here] = jnp.transpose(piece)
            return carry

        lax.fori_loop(0, raw.shape[2] // LANE, turn, 0, unroll=16)
        lax.fori_loop(0, first, clear, 0)
        lax.fori_loop(first + used, window // LANE, clear, 0)


def row_scale(stay_ref, weights, scale_ref):
    rows = stay_ref.shape[1]
    ones = jnp.ones((16, rows), BF16)
    total = jnp.zeros((8, rows), F32)
    for d in range(weights.shape[0] // rows):
        total += jnp.dot(ones, weights[d * rows : (d + 1) * rows, :], preferred_element_type=F32)[0:8]
    scale_ref[...] = (1.0 - stay_ref[...]) / total[0:1]


def kernel(
    start_ref, stay_ref, scale_ref, weights,
    out_ref, ritz_ref,
    images, xbuf, left_ref, current, acc,
    sums,
    bulk_send, bulk_recv, row_send, row_recv, sum_send, sum_recv,
):
    count, rows = start_ref.shape
    reach = weights.shape[0] // (2 * rows)
    devices = lax.axis_size("grp") * lax.axis_size("st")
    members = lax.axis_size("st")
    chain = lax.axis_index("grp") * members + lax.axis_index("st")
    at = coordinates()
    groups = [group(at, names) for names in PHASES]

    x = at["x"]

    def chained(by):
        there = lax.rem(chain + by + devices, devices)
        return (there // members, there % members)

    right = device_of({**at, "x": (x + 1) % 4})
    left = device_of({**at, "x": (x + 3) % 4})
    following, preceding = chained(4), chained(-4)
    across = device_of({**at, "x": (x + 2) % 4})
    neighbours = (right, left, across, following, preceding)

    barrier = pltpu.get_barrier_semaphore()
    for device in neighbours:
        pl.semaphore_signal(barrier, inc=1, device_id=device, device_id_type=MESH)
    for device in [device for _, _, others in groups for device in others]:
        pl.semaphore_signal(barrier, inc=1, device_id=device, device_id_type=MESH)

    def pick(condition, first, second):
        return jnp.where(condition, reach + first, reach + second)

    slots = (
        reach,
        pick(x == 0, 3, -1),
        pick(x < 3, 1, -3),
        pick(x < 2, 2, -2),
        reach - 4,
        reach + 4,
        pick(x == 0, -1, 3),
        pick(x == 3, 1, -3),
        pick(x < 2, -2, 2),
    )
    half = count // 2

    def remote(src, dst, send_sem, recv_sem, device):
        return pltpu.make_async_remote_copy(
            src_ref=src, dst_ref=dst, send_sem=send_sem, recv_sem=recv_sem, device_id=device, device_id_type=MESH
        )

    def spread(parity):
        return [
            remote(images.at[parity, 0], images.at[parity, to], bulk_send.at[k], bulk_recv.at[parity, k], device)
            for k, to, device in ((0, 4, following), (1, 5, preceding), (2, 1, right), (3, 2, left))
        ]

    def onward(parity):
        return [
            remote(
                images.at[parity, src, pl.ds(first, half)],
                images.at[parity, 3, pl.ds(first, half)],
                bulk_send.at[k],
                bulk_recv.at[parity, k],
                device,
            )
            for k, src, first, device in ((4, 1, 0, right), (5, 2, half, left))
        ]

    def arrived(parity, k, block, part=None):
        ref = images.at[parity, block] if part is None else images.at[parity, block, part]
        pltpu.make_async_copy(ref, ref, bulk_recv.at[parity, k]).wait()

    before, after = 4, 5
    along = [
        remote(xbuf.at[jnp.where(x >= 2, before, after)], xbuf.at[8], row_send.at[2], row_recv.at[2], across),
        remote(xbuf.at[jnp.where(x == 3, before, after)], xbuf.at[6], row_send.at[0], row_recv.at[0], right),
        remote(xbuf.at[jnp.where(x >= 1, before, after)], xbuf.at[7], row_send.at[1], row_recv.at[1], left),
    ]

    images[0, 0] = start_ref[...]
    row8 = lax.broadcasted_iota(jnp.int32, (count, 8 * count), 0)
    lane8 = lax.broadcasted_iota(jnp.int32, (count, 8 * count), 1)
    kept = jnp.logical_or(lane8 // 32 < 2, lane8 // 32 == 4)
    left_ref[...] = jnp.where(jnp.logical_and(kept, lane8 % 32 == row8), F32(1), F32(0)).astype(BF16)
    pl.semaphore_wait(barrier, len(neighbours) + sum(len(others) for _, _, others in groups))
    for copy in spread(0):
        copy.start()
    arrived(0, 2, 1)
    arrived(0, 3, 2)
    for copy in onward(0):
        copy.start()

    def stored(slot):
        return weights[pl.ds(pl.multiple_of(slot * rows, rows), rows), :]

    def product(block):
        there = chain + (slots[block] - reach)
        valid = jnp.where(jnp.logical_and(there >= 0, there < devices), F32(1), F32(0)).astype(BF16)
        return jnp.dot(xbuf[block] * valid, stored(slots[block]), preferred_element_type=F32)

    def orthonormal(image):
        ih, im, il = split3(image)
        right = jnp.concatenate([ih, im, ih, im, il, ih, il, im], axis=0)
        return jnp.dot(left_ref[...], right, preferred_element_type=F32)

    lane8 = lax.broadcasted_iota(jnp.int32, (8, LANE), 1) // 32
    lane32 = lax.broadcasted_iota(jnp.int32, (count, LANE), 1) // 32

    def packed_product(left3, right3):
        left = jnp.concatenate(left3, axis=0)
        right = jnp.concatenate([piece for piece in right3 for _ in range(4)], axis=0)
        terms = lax.dot_general(left, right, (((1,), (1,)), ((), ())), preferred_element_type=F32)
        full = tree_sum(terms[32 * a : 32 * a + 32, LANE * b : LANE * b + LANE] for a in (2, 1, 0) for b in (2, 1, 0))
        tile = full[0:8]
        for q in range(1, 4):
            tile = jnp.where(lane8 == q, full[8 * q : 8 * q + 8], tile)
        return tile * (1.0 / (rows * devices))

    def unpacked(tile):
        return [tile] + [pltpu.roll(tile, LANE - 32 * q, 1) for q in range(1, 4)]

    stages = len(groups)
    cross = 2 * stages

    def send_all(stage, base, tile):
        place, _, others = groups[stage]
        own_slot = sums.at[base + stage, place]
        own_slot[...] = tile
        for device in others:
            pltpu.make_async_remote_copy(
                src_ref=own_slot,
                dst_ref=own_slot,
                send_sem=sum_send.at[base + stage],
                recv_sem=sum_recv.at[base + stage],
                device_id=device,
                device_id_type=MESH,
            ).start()

    def wait_all(stage, base, sem):
        part = sums.at[base + stage, pl.ds(0, len(groups[stage][2]))]
        pltpu.make_async_copy(part, part, sem.at[base + stage]).wait()

    def received(stage, base):
        wait_all(stage, base, sum_recv)
        return tree_sum(sums[base + stage, i] for i in range(groups[stage][1]))

    def one_step(t, carry):
        parity = t % 2
        final = t == ITERS - 1
        arrived(parity, 0, 4)
        arrived(parity, 1, 5)
        xbuf[4] = orthonormal(images[parity, 4]).astype(BF16)
        xbuf[5] = orthonormal(images[parity, 5]).astype(BF16)
        for copy in along:
            copy.start()
        updated = orthonormal(images[parity, 0])
        current[...] = updated
        xbuf[0] = updated.astype(BF16)
        acc[...] = product(0) + product(4) + product(5)
        xbuf[1] = orthonormal(images[parity, 1]).astype(BF16)
        xbuf[2] = orthonormal(images[parity, 2]).astype(BF16)
        acc[...] += product(1) + product(2)
        arrived(parity, 4, 3, pl.ds(0, half))
        arrived(parity, 5, 3, pl.ds(half, half))
        xbuf[3] = orthonormal(images[parity, 3]).astype(BF16)
        acc[...] += product(3)
        for k, block in ((0, 6), (1, 7), (2, 8)):
            pltpu.make_async_copy(xbuf.at[block], xbuf.at[block], row_recv.at[k]).wait()
        acc[...] += product(6) + product(7) + product(8)
        image = stay_ref[...] * current[...] + scale_ref[...] * acc[...]
        images[1 - parity, 0] = image
        pieces = split3(image)
        base = parity * stages
        tile = packed_product(pieces, pieces)
        for copy in spread(parity) + onward(parity) + along:
            copy.wait_send()
        send_all(0, base, tile)

        @pl.when(jnp.logical_not(final))
        def _():
            for copy in spread(1 - parity):
                copy.start()

        @pl.when(final)
        def _():
            send_all(0, cross, packed_product(split3(current[...]), pieces))

        for stage in range(1, stages):
            send_all(stage, base, received(stage - 1, base))

            @pl.when(final)
            def _(stage=stage):
                send_all(stage, cross, received(stage - 1, cross))

        @pl.when(jnp.logical_not(final))
        def _():
            arrived(1 - parity, 2, 1)
            arrived(1 - parity, 3, 2)
            for copy in onward(1 - parity):
                copy.start()

        gram = unpacked(received(stages - 1, base))
        high, mid, low = (piece.astype(F32) for piece in split3(inverse_factor(gram)))
        left_a = jnp.where(lane32 < 2, high, mid)
        left_b = jnp.where(lane32 == 0, high, jnp.where(lane32 == 2, mid, low))
        left_ref[...] = jnp.concatenate([left_a, left_b], axis=1).astype(BF16)
        for stage in range(stages):
            wait_all(stage, base, sum_send)
        return carry

    lax.fori_loop(0, ITERS, one_step, 0)

    out_ref[...] = orthonormal(images[ITERS % 2, 0])
    ritz = unpacked(received(stages - 1, cross))
    for q in range(4):
        ritz_ref[8 * q : 8 * q + 8, :] = ritz[q][:, 0:32]
    for stage in range(stages):
        wait_all(stage, cross, sum_send)


def shards(start_vectors, stay, band_blocks, band_start, band_width):
    count, rows = start_vectors.shape
    span = band_blocks.shape[1]
    blocks = band_start.shape[0]
    reach = span // (2 * rows)
    window = 2 * reach + 1
    vmem = pl.BlockSpec(memory_space=pltpu.VMEM)
    most = max(math.prod(SIZES[name] for name in names) for names in PHASES)
    stay = stay.reshape(1, rows)
    hbm = pl.BlockSpec(memory_space=pl.ANY)

    def held(array):
        return pltpu.with_memory_space_constraint(array, pltpu.HBM)

    weights = pl.pallas_call(
        align,
        out_shape=pltpu.VMEM((window * rows, rows), BF16),
        in_specs=[hbm, hbm, hbm],
        out_specs=vmem,
        scratch_shapes=[
            pltpu.VMEM((blocks, rows // blocks, span), BF16),
            pltpu.SMEM((blocks,), jnp.int32),
            pltpu.SMEM((blocks,), jnp.int32),
            pltpu.SemaphoreType.DMA((2 * blocks,)),
            pltpu.SemaphoreType.DMA((2,)),
        ],
        compiler_params=pltpu.CompilerParams(vmem_limit_bytes=24 * 1024 * 1024),
        name="align",
    )(held(band_start), held(band_width), held(band_blocks))
    weights = pltpu.with_memory_space_constraint(weights, pltpu.VMEM)
    scale = pl.pallas_call(
        row_scale,
        out_shape=jax.ShapeDtypeStruct((1, rows), F32),
        in_specs=[vmem, vmem],
        out_specs=vmem,
        compiler_params=pltpu.CompilerParams(vmem_limit_bytes=8 * 1024 * 1024),
        name="row_scale",
    )(stay, weights)
    return pl.pallas_call(
        kernel,
        out_shape=(jax.ShapeDtypeStruct((count, rows), F32), jax.ShapeDtypeStruct((count, count), F32)),
        in_specs=[vmem, vmem, vmem, vmem],
        out_specs=(vmem, vmem),
        scratch_shapes=[
            pltpu.VMEM((2, 6, count, rows), F32),
            pltpu.VMEM((window, count, rows), BF16),
            pltpu.VMEM((count, 8 * count), BF16),
            pltpu.VMEM((count, rows), F32),
            pltpu.VMEM((count, rows), F32),
            pltpu.VMEM((3 * len(PHASES), most, 8, LANE), F32),
            pltpu.SemaphoreType.DMA((6,)),
            pltpu.SemaphoreType.DMA((2, 6)),
            pltpu.SemaphoreType.DMA((3,)),
            pltpu.SemaphoreType.DMA((3,)),
            pltpu.SemaphoreType.DMA((3 * len(PHASES),)),
            pltpu.SemaphoreType.DMA((3 * len(PHASES),)),
        ],
        compiler_params=pltpu.CompilerParams(
            collective_id=0, has_side_effects=True, vmem_limit_bytes=12 * 1024 * 1024
        ),
        name="subspace",
    )(start_vectors, stay, scale, weights)


def solution(mesh):
    placed = (
        P(None, ("grp", "st")),
        P(("grp", "st")),
        P(("grp", "st"), None),
        P(("grp", "st")),
        P(("grp", "st")),
    )
    return jax.shard_map(
        shards, mesh=mesh, in_specs=placed, out_specs=(P(None, ("grp", "st")), P()), check_vma=False
    )
```
